256 devices in a mesh: ctx: 64 (over x, z, core), tp: 4 (over y).
Axes of the slice: x: 4, y: 4, z: 8, core: 2. Of those that a mesh axis runs over, the one named last changes fastest.
Arguments:
- mamba_x: bfloat16 [8192, 8192], P('ctx', 'tp'), may hold values from -6 to 6
- bc_in: bfloat16 [8192, 2, 512], P('ctx', None, 'tp'), may hold values from -6 to 6
- gate_z: bfloat16 [8192, 8192], P('ctx', 'tp'), may hold values from -24 to 24
- conv_x_weight: bfloat16 [4, 8192], P(None, 'tp'), may hold values from -3 to 3
- conv_x_bias: float32 [8192], P('tp'), may hold values from -3 to 3
- conv_bc_weight: bfloat16 [4, 2, 512], P(None, None, 'tp'), may hold values from -3 to 3
- conv_bc_bias: float32 [2, 512], P(None, 'tp'), may hold values from -3 to 3
- decay_log: float32 [8192, 128], P('ctx', 'tp'), may hold values from -1 to 0
- step_size: float32 [8192, 128], P('ctx', 'tp'), may hold values from 0.01 to 0.1
- d_skip: float32 [128], P('tp'), may hold values from 0.5 to 2
- norm_gain: float32 [8192], P('tp'), may hold values from 0.5 to 1.5
- queries: bfloat16 [8192, 64, 128], P('ctx', 'tp'), may hold values from -8 to 8
- attn_keys: bfloat16 [8192, 8, 128], P('ctx', 'tp'), may hold values from -4 to 4
- attn_values: bfloat16 [8192, 8, 128], P('ctx', 'tp'), may hold values from -6 to 6
Outputs:
- mamba_out: float32 [8192, 8192], P(('ctx', 'tp'))
- attn_out: bfloat16 [8192, 64, 128], P('ctx', 'tp')
The draws below stay inside these ranges and needn't reach their ends.
All inputs are finite; a program needn't handle non-finite values.
Results may differ from the reference program's by a relative error of at most 0.006.
Values may be sent and summed in bfloat16 or wider, within the bound.
A program may use at most 192 MiB of HBM per device.

```python
import math
import jax
import jax.numpy as jnp
from jax import lax

TOK_DEV = 128
QH = 64
KVH = 8
HD = 128
STATE_SPACE_HEADS = 128
MP = 64
NS = 128
MG = 4
CONV_K = 4
SEQUENCE_TOKENS = 8192


def draw_decay_log(key, part):
    key = jax.random.fold_in(key, 3)
    complete_keys = jax.random.split(key, 6)
    head_order = jax.random.permutation(complete_keys[0], STATE_SPACE_HEADS)
    fast_heads = head_order < STATE_SPACE_HEADS // 2
    fast_block_log = jnp.exp(jax.random.uniform(complete_keys[1], (STATE_SPACE_HEADS,), jnp.float32, math.log(0.7), math.log(1.2)))
    fast_rate = fast_block_log / TOK_DEV
    slow_rate = jnp.exp(jax.random.uniform(complete_keys[2], (STATE_SPACE_HEADS,), jnp.float32, math.log(0.05 / SEQUENCE_TOKENS), math.log(0.5 / SEQUENCE_TOKENS)))
    head_speed = jnp.where(fast_heads, fast_rate, slow_rate)
    block_spread = jnp.where(fast_heads, 0.25, 0.7)
    block_draw = jax.random.uniform(complete_keys[3], (SEQUENCE_TOKENS // TOK_DEV, STATE_SPACE_HEADS), jnp.float32, -1.0, 1.0)
    block_multiplier = jnp.exp(block_draw * block_spread[None, :])
    block_multiplier = jnp.repeat(block_multiplier, TOK_DEV, axis=0)
    token_multiplier = jnp.exp(jax.random.uniform(complete_keys[4], (SEQUENCE_TOKENS, STATE_SPACE_HEADS), jnp.float32, -0.5, 0.5))
    spike_keys = jax.random.split(complete_keys[5], 2)
    spike_rows = jax.random.randint(spike_keys[0], (3,), 0, SEQUENCE_TOKENS)
    spike_penalty = jnp.log(1.0 - jax.random.uniform(spike_keys[1], (3, STATE_SPACE_HEADS), jnp.float32, 0.2, 0.4))
    token_positions = jnp.arange(SEQUENCE_TOKENS, dtype=jnp.int32)
    spike_matched = token_positions[:, None] == spike_rows[None, :]
    spike_sum_total = jnp.sum(jnp.where(spike_matched[:, :, None], spike_penalty[None, :, :], 0.0), axis=1)
    return jnp.clip(-head_speed[None, :] * block_multiplier * token_multiplier + spike_sum_total, -1.0, 0.0)


def draw_gate_z(key, part):
    key = jax.random.fold_in(key, 5)
    complete_keys = jax.random.split(key, 3)
    channel_scale = jnp.exp(jax.random.uniform(complete_keys[0], (STATE_SPACE_HEADS * MP,), jnp.float32, 0.0, math.log(10.0)))
    token_scale = jnp.exp(jax.random.uniform(complete_keys[1], (SEQUENCE_TOKENS, 1), jnp.float32, 0.0, math.log(3.0)))
    base_vals = jax.random.truncated_normal(complete_keys[2], -4.0, 4.0, (SEQUENCE_TOKENS, STATE_SPACE_HEADS * MP), jnp.float32)
    return jnp.clip(base_vals * channel_scale[None, :] * token_scale / 4.0, -24.0, 24.0).astype(jnp.bfloat16)


def attention_pair(key):
    complete_keys = jax.random.split(jax.random.fold_in(key, 11), 2)
    query_vals = jax.random.truncated_normal(complete_keys[0], -4.0, 4.0, (SEQUENCE_TOKENS, QH, HD), jnp.float32)
    key_vals = jax.random.truncated_normal(complete_keys[1], -4.0, 4.0, (SEQUENCE_TOKENS, KVH, HD), jnp.float32)
    return (query_vals, key_vals)


def draw_queries(key, part):
    return attention_pair(key)[0].astype(jnp.bfloat16)


def draw_attn_keys(key, part):
    return attention_pair(key)[1].astype(jnp.bfloat16)


def block_scale(key, dims, cuts, low, largest):
    level, own = 1.0, jax.random.fold_in(key, 6)
    for position, shards_of in cuts:
        draws = jnp.exp(jax.random.uniform(jax.random.fold_in(own, position), (shards_of,), jnp.float32, low / len(cuts), largest / len(cuts)))
        level = level * jnp.repeat(draws, dims[position] // shards_of).reshape([-1 if axis == position else 1 for axis in range(len(dims))])
    return level


def bell_draw(own_key, shape, scale, most, cuts=(), kind=jnp.bfloat16):
    values = scale * jax.random.normal(own_key, shape, jnp.float32)
    if cuts:
        values = values * block_scale(own_key, shape, cuts, -0.22, 0.18)
    return jnp.clip(values, -most, most).astype(kind)


def setup_inputs(seed: int = 0) -> dict:
    keys = jax.random.split(jax.random.key(seed), 15)
    mamba_x = bell_draw(keys[0], (SEQUENCE_TOKENS, STATE_SPACE_HEADS * MP), 1.0, 6.0, ((0, 64), (1, 4)))
    bc_in = bell_draw(keys[1], (SEQUENCE_TOKENS, 2, MG * NS), 1.0, 6.0, ((0, 64), (2, 4)))
    gate_z = draw_gate_z(jax.random.fold_in(keys[14], 71), 0)
    conv_x_weight = bell_draw(keys[3], (CONV_K, STATE_SPACE_HEADS * MP), CONV_K ** -0.5, 3.0, ((1, 4),))
    conv_x_bias = bell_draw(keys[4], (STATE_SPACE_HEADS * MP,), 0.5, 3.0, ((0, 4),), jnp.float32)
    conv_bc_weight = bell_draw(keys[5], (CONV_K, 2, MG * NS), CONV_K ** -0.5, 3.0, ((2, 4),))
    conv_bc_bias = bell_draw(keys[6], (2, MG * NS), 0.5, 3.0, ((1, 4),), jnp.float32)
    decay_log = draw_decay_log(jax.random.fold_in(keys[14], 71), 0)
    step_size = jnp.clip(jnp.exp(math.log(0.1) - 2.3025851 * jax.random.uniform(keys[8], (SEQUENCE_TOKENS, STATE_SPACE_HEADS), jnp.float32) ** block_scale(keys[8], (SEQUENCE_TOKENS, STATE_SPACE_HEADS), ((0, 64), (1, 4)), -0.2, 0.2)), 0.01, 0.1)
    d_skip = jnp.clip(jnp.exp(math.log(2.0) - 1.3862944 * jax.random.uniform(keys[9], (STATE_SPACE_HEADS,), jnp.float32) ** block_scale(keys[9], (STATE_SPACE_HEADS,), ((0, 4),), -0.2, 0.2)), 0.5, 2.0)
    norm_gain = jnp.clip(1.0 + 0.1 * jax.random.normal(keys[10], (STATE_SPACE_HEADS * MP,), jnp.float32), 0.5, 1.5)
    queries = draw_queries(jax.random.fold_in(keys[14], 71), 0)
    attn_keys = draw_attn_keys(jax.random.fold_in(keys[14], 71), 0)
    attn_values = bell_draw(keys[13], (SEQUENCE_TOKENS, KVH, HD), 1.0, 6.0, ((0, 64), (1, 4)))
    return {"mamba_x": mamba_x, "bc_in": bc_in, "gate_z": gate_z, "conv_x_weight": conv_x_weight, "conv_x_bias": conv_x_bias, "conv_bc_weight": conv_bc_weight, "conv_bc_bias": conv_bc_bias, "decay_log": decay_log, "step_size": step_size, "d_skip": d_skip, "norm_gain": norm_gain, "queries": queries, "attn_keys": attn_keys, "attn_values": attn_values}


NEG_BIG = -1e+30
NORM_EPS = 1e-05

def causal_conv(window, conv_weight, conv_bias):
    kernel_taps = conv_weight.shape[0]
    out_len = window.shape[0] - kernel_taps + 1
    summed = jnp.broadcast_to(conv_bias.astype(jnp.float32)[None, :], (out_len, window.shape[1]))
    for offset in range(kernel_taps):
        summed = summed + window[offset:offset + out_len].astype(jnp.float32) * conv_weight[offset].astype(jnp.float32)[None, :]
    return jax.nn.silu(summed).astype(jnp.bfloat16)

def ssd_local(xheads, b_state, c_state, decay_block, step_block):
    precise = lax.Precision.HIGHEST
    block_len = xheads.shape[0]
    per_group = xheads.shape[1] // b_state.shape[1]
    cum_decay = jnp.cumsum(decay_block, axis=0)
    cum_cols = cum_decay.T
    causal = jnp.arange(block_len, dtype=jnp.int32)[:, None] >= jnp.arange(block_len, dtype=jnp.int32)[None, :]
    pair_dots = jnp.einsum('tgn,sgn->gts', c_state, b_state, precision=precise)
    head_dots = jnp.repeat(pair_dots, per_group, axis=0)
    gap_vals = jnp.where(causal[None], cum_cols[:, :, None] - cum_cols[:, None, :], 0.0)
    mixing = jnp.where(causal[None], head_dots * jnp.exp(gap_vals) * step_block.T[:, None, :], 0.0)
    intra_y = jnp.einsum('hts,shp->thp', mixing, xheads, precision=precise)
    end_weight = jnp.exp(cum_decay[-1][None, :] - cum_decay) * step_block
    b_heads = jnp.repeat(b_state, per_group, axis=1)
    c_heads = jnp.repeat(c_state, per_group, axis=1)
    local_state = jnp.einsum('sh,shp,shn->hpn', end_weight, xheads, b_heads, precision=precise)
    return (intra_y, cum_decay, c_heads, local_state, jnp.exp(cum_decay[-1]))

def mamba_layer(mamba_x, bc_in, gate_z, conv_x_weight, conv_x_bias, conv_bc_weight, conv_bc_bias, decay_log, step_size, d_skip, norm_gain):
    seq_len = mamba_x.shape[0]
    kernel_taps = conv_x_weight.shape[0]
    joined = jnp.concatenate([mamba_x, bc_in.reshape(seq_len, -1)], axis=1)
    window = jnp.concatenate([jnp.zeros((kernel_taps - 1, joined.shape[1]), jnp.bfloat16), joined], axis=0)
    conv_weight = jnp.concatenate([conv_x_weight, conv_bc_weight.reshape(kernel_taps, -1)], axis=1)
    conv_bias = jnp.concatenate([conv_x_bias, conv_bc_bias.reshape(-1)])
    convolved = causal_conv(window, conv_weight, conv_bias)
    channels = STATE_SPACE_HEADS * MP
    num_blocks = seq_len // TOK_DEV
    xheads = convolved[:, :channels].reshape(num_blocks, TOK_DEV, STATE_SPACE_HEADS, MP).astype(jnp.float32)
    bc_conv = convolved[:, channels:].reshape(num_blocks, TOK_DEV, 2, MG, NS).astype(jnp.float32)
    decays = decay_log.reshape(num_blocks, TOK_DEV, STATE_SPACE_HEADS)
    step_blocks = step_size.reshape(num_blocks, TOK_DEV, STATE_SPACE_HEADS)

    def advance(carry_state, pieces):
        x_blk, bc_blk, dec_blk, stp_blk = pieces
        intra_y, cum_decay, c_heads, local_state, block_decay = ssd_local(x_blk, bc_blk[:, 0], bc_blk[:, 1], dec_blk, stp_blk)
        carried = jnp.exp(cum_decay)[:, :, None] * jnp.einsum('hpn,thn->thp', carry_state, c_heads, precision=lax.Precision.HIGHEST)
        y_blk = intra_y + carried + d_skip[None, :, None] * x_blk
        return (block_decay[:, None, None] * carry_state + local_state, y_blk)
    start_state = jnp.zeros((STATE_SPACE_HEADS, MP, NS), jnp.float32)
    final_state, ssm_y = lax.scan(advance, start_state, (xheads, bc_conv, decays, step_blocks))
    gated_y = ssm_y.reshape(seq_len, channels) * jax.nn.silu(gate_z.astype(jnp.float32))
    grouped = gated_y.reshape(seq_len, MG, channels // MG)
    normed = (grouped * lax.rsqrt(lax.optimization_barrier(jnp.mean(grouped * grouped, axis=-1, keepdims=True)) + NORM_EPS)).reshape(seq_len, channels)
    return (normed * norm_gain[None, :]).astype(jnp.float32)

def attention_core(queries, attn_keys, attn_values):
    seq_len = queries.shape[0]
    block_rows = min(TOK_DEV, 128)
    per_kv = QH // KVH
    score_scale = 1.0 / math.sqrt(HD)
    keys_f = attn_keys.astype(jnp.float32)
    values_f = attn_values.astype(jnp.float32)
    key_pos = jnp.arange(seq_len, dtype=jnp.int32)

    def one_block(block_index):
        first_row = (block_index * block_rows).astype(jnp.int32)
        q_rows = lax.dynamic_slice_in_dim(queries, first_row, block_rows, 0).astype(jnp.float32).reshape(block_rows, KVH, per_kv, HD)
        scores = jnp.einsum('qkgd,tkd->kgqt', q_rows, keys_f) * score_scale
        q_pos = first_row + jnp.arange(block_rows, dtype=jnp.int32)
        visible = key_pos[None, None, None, :] <= q_pos[None, None, :, None]
        row_peak = lax.optimization_barrier(jnp.max(jnp.where(visible, scores, NEG_BIG), axis=-1))
        exp_vals = jnp.where(visible, jnp.exp(scores - row_peak[..., None]), 0.0)
        denominator = lax.optimization_barrier(jnp.sum(exp_vals, axis=-1))
        rounded = lax.optimization_barrier(exp_vals.astype(jnp.bfloat16)).astype(jnp.float32)
        mixed = jnp.einsum('kgqt,tkd->kgqd', rounded, values_f)
        result = (mixed / denominator[..., None]).astype(jnp.bfloat16)
        return result.transpose(2, 0, 1, 3).reshape(block_rows, QH, HD)
    blocks_out = lax.map(one_block, jnp.arange(seq_len // block_rows, dtype=jnp.int32))
    return blocks_out.reshape(seq_len, QH, HD)

def reference(mamba_x, bc_in, gate_z, conv_x_weight, conv_x_bias, conv_bc_weight, conv_bc_bias, decay_log, step_size, d_skip, norm_gain, queries, attn_keys, attn_values):
    return (mamba_layer(mamba_x, bc_in, gate_z, conv_x_weight, conv_x_bias, conv_bc_weight, conv_bc_bias, decay_log, step_size, d_skip, norm_gain), attention_core(queries, attn_keys, attn_values))
```

```python
import functools
import math

import jax
import jax.numpy as jnp
from jax import lax
from jax.experimental import pallas as pl
from jax.experimental.pallas import tpu as pltpu
from jax.sharding import PartitionSpec as P

MESH = pl.DeviceIdType.MESH
F32 = jnp.float32
BF16 = jnp.bfloat16
EXACT = lax.Precision.HIGHEST

TOK = 128
NS = 128
PAIRS = 16
TP = 4
ROWS = 1024
KT = 1024
RC = 256
NEG = -1e30
NORM_EPS = 1e-05
MSG = 144

NT = (((1,), (1,)), ((), ()))


def dot(a, b, dims=(((1,), (0,)), ((), ())), precision=None):
    return lax.dot_general(a, b, dims, precision=precision, preferred_element_type=F32)


def silu(v):
    return v * jax.nn.sigmoid(v)


def body(
    mx, bc, gate, wx, bx, wbc, bbc, decay, step, dskip, gain, q2, kvp,
    out, att,
    hx, hbc, win, xc, bcv, btr, cumt, stept, wend, ecum, gmat, ylocal,
    smsg, rmsg, pre, clog, xsend, xrecv, isend, irecv,
    qb, kvg, acc, mrun, obuf, nbuf, nrecv,
    loc, sws, swr, xs, xr, rs, rr, cs, cr, a1s, a1r, xxs, xxr, a2s, a2r, tps, tpr, os_, or_,
):
    ctx, tp = lax.axis_index("ctx"), lax.axis_index("tp")
    x, r = ctx // 16, ctx % 16
    z, c = r // 2, r % 2
    hi = x // 2
    px = 3 - x
    pr = x + hi * (3 - 2 * x)
    xn = x + 1 - 2 * (x % 2)
    zp, zm = (z + 1) % 8, (z + 7) % 8

    def dev(x_, r_):
        return (x_ * 16 + r_, tp)

    def remote(src, dst, s, rv, to):
        return pltpu.make_async_remote_copy(
            src_ref=src, dst_ref=dst, send_sem=s, recv_sem=rv, device_id=to, device_id_type=MESH
        )

    bar = pltpu.get_barrier_semaphore()

    def greet(to):
        pl.semaphore_signal(bar, inc=1, device_id=to, device_id_type=MESH)

    def greet_group(j, carry):
        greet(dev(x, (r + j) % 16))
        return carry

    lax.fori_loop(1, 16, greet_group, 0)
    for j in range(1, 4):
        greet(dev((x + j) % 4, r))
        greet((ctx, (tp + j) % 4))
    greet(((ctx + 1) % 64, tp))
    greet(((ctx + 63) % 64, tp))
    pl.semaphore_wait(bar, 23)

    partner = dev(px, r)
    mine = kvg.at[r, pr]
    after = ((ctx + 1) % 64, tp)
    kv_swap = remote(kvp.at[1 - hi], kvg.at[r, pr, hi], sws.at[0], swr.at[0], partner)
    kv_swap.start()
    halo_x = remote(mx.at[TOK - 16 : TOK], hx, sws.at[1], swr.at[1], after)
    halo_x.start()
    halo_bc = remote(bc.at[TOK - 16 : TOK], hbc, sws.at[2], swr.at[2], after)
    halo_bc.start()
    q_swap = remote(q2.at[1 - hi], qb.at[hi], sws.at[3], swr.at[3], partner)
    q_swap.start()
    kv_own = pltpu.make_async_copy(kvp.at[hi], kvg.at[r, pr, hi], loc.at[0])
    kv_own.start()
    q_own = pltpu.make_async_copy(q2.at[hi], qb.at[hi], loc.at[1])
    q_own.start()

    rows = lax.broadcasted_iota(jnp.int32, (TOK, TOK), 0)
    cols = lax.broadcasted_iota(jnp.int32, (TOK, TOK), 1)
    causal = rows >= cols
    tril = causal.astype(F32)
    cum = dot(tril, decay[...], precision=EXACT)
    eye = (lax.broadcasted_iota(jnp.int32, (32, 32), 0) == lax.broadcasted_iota(jnp.int32, (32, 32), 1)).astype(F32)
    cumt[...] = dot(eye, cum, NT, EXACT)
    stept[...] = dot(eye, step[...], NT, EXACT)
    last = cum[TOK - 1 : TOK]
    wend[...] = jnp.exp(last - cum) * step[...]
    ecum[...] = cum

    ring_sends = []

    def ring(slot, d, s, q):
        k = (d * 4 + s) * 2 + q
        copy = remote(slot, slot, rs.at[k], rr.at[k], dev(x, (zp if d == 0 else zm) * 2 + c))
        copy.start()
        ring_sends.append(copy)
        return copy

    def to_core(slot, k):
        copy = remote(slot, slot, cs.at[k], cr.at[k], dev(x, z * 2 + 1 - c))
        copy.start()
        ring_sends.append(copy)

    hops = {}
    kv_own.wait()
    kv_swap.wait()
    x_swap = remote(mine, mine, xs.at[0], xr.at[0], dev(xn, r))
    x_swap.start()
    hops[0, 0, 0] = ring(mine, 0, 0, 0)
    hops[1, 0, 0] = ring(mine, 1, 0, 0)
    to_core(mine, 0)

    halo_x.wait()
    halo_bc.wait()
    first = ctx > 0

    def conv(chunk, before, weight, bias):
        win[0:16] = jnp.where(first, before.astype(F32), 0.0)
        win[16:144] = chunk.astype(F32)
        w = weight.astype(F32)
        total = jnp.broadcast_to(bias, (TOK, 128))
        for k in range(4):
            total = total + win[13 + k : 13 + k + TOK] * w[k : k + 1]
        return silu(total).astype(BF16)

    for k in range(2):
        cut = slice(k * 128, k * 128 + 128)
        bcv[k] = conv(bc[:, cut], hbc[:, cut], wbc[:, cut], bbc[:, cut])

    def conv_pair(p, carry):
        cut = pl.ds(pl.multiple_of(p * 128, 128), 128)
        xc[p] = conv(mx[:, cut], hx[:, cut], wx[:, cut], bx[:, cut])
        return carry

    lax.fori_loop(0, PAIRS, conv_pair, 0)
    btr[...] = bcv[0].astype(F32).T.astype(BF16)
    gmat[...] = dot(bcv[1], bcv[0], NT)

    x_swap.wait()
    theirs = kvg.at[r, 1 - pr]
    hops[0, 0, 1] = ring(theirs, 0, 0, 1)
    hops[1, 0, 1] = ring(theirs, 1, 0, 1)
    to_core(theirs, 1)

    lane_head = lax.broadcasted_iota(jnp.int32, (32, 128), 1) // 64
    head_row = lax.broadcasted_iota(jnp.int32, (32, 128), 0)

    def spread(p):
        return (head_row == 2 * p + lane_head).astype(F32)

    row16 = lax.broadcasted_iota(jnp.int32, (16, 128), 0)

    def log_rows(v):
        v = jnp.broadcast_to(v, (16, 128))
        top = v.astype(BF16)
        rest = v - top.astype(F32)
        mid = rest.astype(BF16)
        low = (rest - mid.astype(F32)).astype(BF16)
        zero = jnp.zeros((16, 128), BF16)
        return jnp.where(row16 == 0, top, jnp.where(row16 == 1, mid, jnp.where(row16 == 2, low, zero)))

    def read_log(msg_tail):
        v = msg_tail.astype(F32)
        return v[0:1] + v[1:2] + v[2:3]

    def local_state(p):
        e = spread(p)
        weighted = (xc[p].astype(F32) * dot(wend[...], e, precision=EXACT)).astype(BF16)
        total = dot(ecum[TOK - 8 : TOK], e, precision=EXACT)[7:8]
        return dot(btr[...], weighted).astype(BF16), log_rows(total)

    def state_copy(p):
        return remote(smsg.at[p], rmsg.at[r], a1s.at[p], a1r.at[r], dev(x, p))

    def send_state(j, carry):
        p = (r + j) % 16
        state, logs = local_state(p)
        smsg[p, 0:NS] = state
        smsg[p, NS:MSG] = logs
        state_copy(p).start()
        return carry

    lax.fori_loop(1, 16, send_state, 0)
    state, logs = local_state(r)
    rmsg[r, 0:NS] = state
    rmsg[r, NS:MSG] = logs

    def take_ring(s):
        for q in range(2):
            for d in range(2):
                if s == 3 and q != d:
                    continue
                hops[d, s, q].wait_recv()
                zo = (z + 7 - s) % 8 if d == 0 else (z + s + 1) % 8
                slot = kvg.at[zo * 2 + c, pr if q == 0 else 1 - pr]
                if s < 2 or (s == 2 and q == d):
                    hops[d, s + 1, q] = ring(slot, d, s + 1, q)
                to_core(slot, 2 + s * 4 + q * 2 + d if s < 3 else 14 + q)

    lane = lax.broadcasted_iota(jnp.int32, (TOK, 128), 1)

    def one_head(h, col_log):
        gap = jnp.where(causal, col_log - cumt[pl.ds(h, 1), :], NEG)
        return (gmat[...] * jnp.exp(gap) * stept[pl.ds(h, 1), :]).astype(BF16)

    def intra(p, carry):
        h = 2 * p
        col0 = dot(ecum[...], (head_row == h).astype(F32), precision=EXACT)
        col1 = dot(ecum[...], (head_row == h + 1).astype(F32), precision=EXACT)
        mixing = jnp.concatenate([one_head(h, col0), one_head(h + 1, col1)], axis=1)
        xp = xc[p]
        zero = jnp.zeros_like(xp)
        stacked = jnp.concatenate([jnp.where(lane < 64, xp, zero), jnp.where(lane < 64, zero, xp)], axis=0)
        skip = dot(jnp.broadcast_to(dskip[...], (8, 32)), spread(p), precision=EXACT)[0:1]
        ylocal[p] = dot(mixing, stacked) + skip * xp.astype(F32)
        return carry

    take_ring(0)
    lax.fori_loop(0, 8, intra, 0)
    take_ring(1)
    lax.fori_loop(8, 16, intra, 0)
    take_ring(2)

    def chain(k, carry):
        state, logs = carry

        @pl.when(k != r)
        def _():
            remote(smsg.at[k], rmsg.at[k], a1s.at[k], a1r.at[k], dev(x, k)).wait_recv()

        pre[k] = state
        clog[k] = jnp.broadcast_to(logs, (8, 128))
        new = read_log(rmsg[k, NS:MSG])
        return jnp.exp(new) * state + rmsg[k, 0:NS].astype(F32), logs + new

    state, logs = lax.fori_loop(0, 16, chain, (jnp.zeros((NS, 128), F32), jnp.zeros((1, 128), F32)))
    xsend[0:NS] = state.astype(BF16)
    xsend[NS:MSG] = log_rows(logs)

    def x_copy(j):
        to = (x + j) % 4
        return remote(xsend, xrecv.at[x], xxs.at[to], xxr.at[x], dev(to, r))

    for j in range(1, 4):
        x_copy(j).start()
    take_ring(3)
    enter = jnp.zeros((NS, 128), F32)
    for j in range(4):

        @pl.when(x != j)
        def _():
            remote(xsend, xrecv.at[j], xxs.at[j], xxr.at[j], dev(j, r)).wait_recv()

    xrecv[x] = xsend[...]
    for j in range(3):
        enter = jnp.where(j < x, jnp.exp(read_log(xrecv[j, NS:MSG])) * enter + xrecv[j, 0:NS].astype(F32), enter)

    def back_copy(k):
        return remote(isend.at[k], irecv.at[r], a2s.at[k], a2r.at[r], dev(x, k))

    def send_back(j, carry):
        k = (r + j) % 16
        isend[k] = (jnp.exp(clog[k, 0:1]) * enter + pre[k]).astype(BF16)
        back_copy(k).start()
        return carry

    lax.fori_loop(1, 16, send_back, 0)
    irecv[r] = (jnp.exp(clog[r, 0:1]) * enter + pre[r]).astype(BF16)

    for k in range(16):
        slot = kvg.at[0, 0]
        remote(slot, slot, cs.at[k], cr.at[k], dev(x, z * 2 + 1 - c)).wait_recv()
    log_scale = math.log2(math.e) / math.sqrt(128)
    ones = jnp.ones((KT, 128), BF16)

    def tile(pos, pk, posk, r0, visible):
        kt = kvg[pl.ds(r0, 8), pk, posk, 0].reshape(KT, 128)
        vt = jnp.concatenate([kvg[pl.ds(r0, 8), pk, posk, 1].reshape(KT, 128), ones], axis=1)
        for i in range(ROWS // RC):
            cut = slice(i * RC, i * RC + RC)
            s = dot(qb[pos, cut], kt, NT)
            if visible is not None:
                s = jnp.where(visible(i, r0), s, NEG)
            old = mrun[cut]
            new = jnp.maximum(old, jnp.max(s, axis=1, keepdims=True))
            p = jnp.exp2((s - jnp.concatenate([new] * (KT // 128), axis=1)) * log_scale)
            fade = jnp.exp2((old - new) * log_scale)
            acc[cut] = acc[cut] * jnp.concatenate([fade, fade], axis=1) + dot(p.astype(BF16), vt)
            mrun[cut] = new

    def seen(i, r0):
        tok = (lax.broadcasted_iota(jnp.int32, (RC, KT), 0) + i * RC) // 8
        key = lax.broadcasted_iota(jnp.int32, (RC, KT), 1) + r0 * 128
        return key <= tok + r * 128

    def attend(pos):
        big = pr + pos * (3 - 2 * pr)
        mrun[...] = jnp.full((ROWS, 128), NEG, F32)
        acc[...] = jnp.zeros((ROWS, 256), F32)

        def whole(it, carry):
            kx, half = it // 2, it % 2
            pk = kx + (kx // 2) * (3 - 2 * kx)
            tile(pos, pk, kx // 2, half * 8, None)
            return carry

        lax.fori_loop(0, 2 * big, whole, 0)

        def edge(it, carry):
            tile(pos, pr, pos, it * 8, seen)
            return carry

        lax.fori_loop(0, r // 8 + 1, edge, 0)
        for i in range(ROWS // RC):
            cut = slice(i * RC, i * RC + RC)
            a = acc[cut]
            obuf[pos, cut] = (a[:, :128] / a[:, 128:]).astype(BF16)

    q_swap.wait()
    q_own.wait()
    attend(1 - hi)
    o_swap = remote(obuf.at[1 - hi], att.at[hi], os_.at[0], or_.at[0], partner)
    o_swap.start()
    attend(hi)
    o_own = pltpu.make_async_copy(obuf.at[hi], att.at[hi], loc.at[2])
    o_own.start()

    def wait_back(j, carry):
        k = (r + j) % 16
        remote(isend.at[k], irecv.at[k], a2s.at[k], a2r.at[k], dev(x, k)).wait_recv()
        return carry

    lax.fori_loop(1, 16, wait_back, 0)

    def row_copy(to):
        return remote(nbuf.at[to], nrecv.at[tp], tps.at[to], tpr.at[tp], (ctx, to))

    def finish(to):
        cut = pl.ds(pl.multiple_of(to * 32, 32), 32)
        crow = bcv[1, cut]
        ex = jnp.exp(ecum[cut])

        def pair(p, square):
            lanes = pl.ds(pl.multiple_of(p * 128, 128), 128)
            carried = dot(crow, irecv[p]) * dot(ex, spread(p), precision=EXACT)
            g = gate[cut, lanes].astype(F32)
            y = (ylocal[p, cut] + carried) * silu(g)
            ylocal[p, cut] = y
            return square + y * y

        square = lax.fori_loop(0, PAIRS, pair, jnp.zeros((32, 128), F32))
        norm = lax.rsqrt(jnp.sum(square, axis=1, keepdims=True) * (1.0 / 2048) + NORM_EPS)

        def scale(p, carry):
            lanes = pl.ds(pl.multiple_of(p * 128, 128), 128)
            nbuf[to, :, lanes] = (ylocal[p, cut] * norm * gain[:, lanes]).astype(BF16)
            return carry

        lax.fori_loop(0, PAIRS, scale, 0)

    def rows_of(j, carry):
        to = (tp + j) % 4
        finish(to)
        row_copy(to).start()
        return carry

    lax.fori_loop(1, 4, rows_of, 0)
    finish(tp)
    nrecv[tp] = nbuf[tp]

    def rows_in(j, carry):
        k = (tp + j) % 4
        remote(nbuf.at[k], nrecv.at[k], tps.at[k], tpr.at[k], (ctx, k)).wait_recv()
        return carry

    lax.fori_loop(1, 4, rows_in, 0)
    for k in range(4):
        out[:, k * 2048 : (k + 1) * 2048] = nrecv[k].astype(F32)

    def left_group(j, carry):
        k = (r + j) % 16
        state_copy(k).wait_send()
        back_copy(k).wait_send()
        return carry

    lax.fori_loop(1, 16, left_group, 0)
    for j in range(1, 4):
        x_copy(j).wait_send()

    def left_rows(j, carry):
        row_copy((tp + j) % 4).wait_send()
        return carry

    lax.fori_loop(1, 4, left_rows, 0)
    for copy in ring_sends:
        copy.wait_send()
    o_own.wait()
    o_swap.wait()


def per_device(
    mamba_x, bc_in, gate_z, conv_x_weight, conv_x_bias, conv_bc_weight, conv_bc_bias,
    decay_log, step_size, d_skip, norm_gain, queries, attn_keys, attn_values,
):
    bc = bc_in.reshape(TOK, 256)
    wbc = conv_bc_weight.reshape(4, 256)
    bbc = conv_bc_bias.reshape(1, 256)
    bx = conv_x_bias.reshape(1, 2048)
    q2 = queries.reshape(TOK, 2, 8, 128).transpose(1, 0, 2, 3).reshape(2, ROWS, 128)
    kvp = jnp.stack([attn_keys, attn_values]).transpose(2, 0, 1, 3)
    vmem = pl.BlockSpec(memory_space=pltpu.VMEM)
    dma = lambda *n: pltpu.SemaphoreType.DMA(n)
    buf = pltpu.VMEM
    out, att = pl.pallas_call(
        body,
        out_shape=(
            jax.ShapeDtypeStruct((32, 8192), F32),
            jax.ShapeDtypeStruct((2, ROWS, 128), BF16),
        ),
        in_specs=[vmem] * 13,
        out_specs=(vmem, vmem),
        scratch_shapes=[
            buf((16, 2048), BF16), buf((16, 256), BF16), buf((144, 128), F32), buf((PAIRS, TOK, 128), BF16),
            buf((2, TOK, 128), BF16), buf((NS, TOK), BF16), buf((32, TOK), F32), buf((32, TOK), F32),
            buf((TOK, 32), F32), buf((TOK, 32), F32), buf((TOK, TOK), F32), buf((PAIRS, TOK, 128), F32),
            buf((16, MSG, 128), BF16), buf((16, MSG, 128), BF16), buf((16, NS, 128), F32), buf((16, 8, 128), F32),
            buf((MSG, 128), BF16), buf((4, MSG, 128), BF16), buf((16, NS, 128), BF16), buf((16, NS, 128), BF16),
            buf((2, ROWS, 128), BF16), buf((16, 2, 2, 2, 128, 128), BF16), buf((ROWS, 256), F32), buf((ROWS, 128), F32),
            buf((2, ROWS, 128), BF16), buf((4, 32, 2048), BF16), buf((4, 32, 2048), BF16),
            dma(3), dma(4), dma(4), dma(1), dma(1), dma(16), dma(16), dma(16), dma(16),
            dma(16), dma(16), dma(4), dma(4), dma(16), dma(16), dma(4), dma(4), dma(1), dma(1),
        ],
        compiler_params=pltpu.CompilerParams(
            collective_id=0, has_side_effects=True, vmem_limit_bytes=48 << 20
        ),
    )(
        mamba_x, bc, gate_z, conv_x_weight, bx, wbc, bbc, decay_log, step_size,
        d_skip.reshape(1, 32), norm_gain.reshape(1, 2048), q2, kvp,
    )
    attn = att.reshape(2, TOK, 8, 128).transpose(1, 0, 2, 3).reshape(TOK, 16, 128)
    return out, attn


def solution(mesh):
    in_specs = (
        P("ctx", "tp"), P("ctx", None, "tp"), P("ctx", "tp"), P(None, "tp"), P("tp"), P(None, None, "tp"),
        P(None, "tp"), P("ctx", "tp"), P("ctx", "tp"), P("tp"), P("tp"), P("ctx", "tp", None),
        P("ctx", "tp", None), P("ctx", "tp", None),
    )
    out_specs = (P(("ctx", "tp"), None), P("ctx", "tp", None))
    return jax.shard_map(per_device, mesh=mesh, in_specs=in_specs, out_specs=out_specs, check_vma=False)
```

```python
import functools
import math

import jax
import jax.numpy as jnp
from jax import lax
from jax.experimental import pallas as pl
from jax.experimental.pallas import tpu as pltpu
from jax.sharding import PartitionSpec as P

MESH = pl.DeviceIdType.MESH
F32 = jnp.float32
BF16 = jnp.bfloat16
EXACT = lax.Precision.HIGHEST

TOK = 128
NS = 128
PAIRS = 16
TP = 4
ROWS = 1024
KT = 1024
RC = 256
NEG = -1e30
NORM_EPS = 1e-05
MSG = 144

NT = (((1,), (1,)), ((), ()))


def dot(a, b, dims=(((1,), (0,)), ((), ())), precision=None):
    return lax.dot_general(a, b, dims, precision=precision, preferred_element_type=F32)


def silu(v):
    return v * jax.nn.sigmoid(v)


def split3(v):
    top = v.astype(BF16)
    rest = v - top.astype(F32)
    mid = rest.astype(BF16)
    low = (rest - mid.astype(F32)).astype(BF16)
    return top, mid, low


def body(
    mx_, bc_, gate_, wx_, bx_, wbc_, bbc_, decay_, step_, dskip_, gain_, q2, kvp,
    out, att,
    mx, bc, gate, wx, bx, wbc, bbc, decay, step, dskip, gain,
    hx, hbc, win, xc, bcv, btr, cumt, stept, cum3, spx, gmat, ylocal, egate,
    other, both, smsg, rmsg, pre, clog, xsend, xrecv, isend, iback, ipass, irecv,
    qb, kvg, acc, mrun, obuf, nbuf, nrecv,
    loc, sws, swr, xs, xr, rs, rr, cs, cr, fs, fr, ms, mr, a1s, a1r, xxs, xxr, a2s, a2r, bs, br, tps, tpr, os_, or_,
):
    ctx, tp = lax.axis_index("ctx"), lax.axis_index("tp")
    x, r = ctx // 16, ctx % 16
    z, c = r // 2, r % 2
    hi = x // 2
    px = 3 - x
    pr = x + hi * (3 - 2 * x)
    xn = x + 1 - 2 * (x % 2)
    zp, zm = (z + 1) % 8, (z + 7) % 8

    def dev(x_, r_):
        return (x_ * 16 + r_, tp)

    def remote(src, dst, s, rv, to):
        return pltpu.make_async_remote_copy(
            src_ref=src, dst_ref=dst, send_sem=s, recv_sem=rv, device_id=to, device_id_type=MESH
        )

    def local(src, dst, k):
        return pltpu.make_async_copy(src, dst, loc.at[k])

    pairs_in = (
        (decay_, decay), (step_, step), (mx_, mx), (bc_, bc), (wx_, wx), (bx_, bx), (wbc_, wbc), (bbc_, bbc),
        (dskip_, dskip), (gate_, gate), (gain_, gain),
    )
    loads = [local(a, b, k) for k, (a, b) in enumerate(pairs_in)]
    for load in loads:
        load.start()
    kv_own = local(kvp.at[hi], kvg.at[r, pr, hi], 11)
    kv_own.start()
    q_own = local(q2.at[hi], qb.at[hi], 12)
    q_own.start()

    bar = pltpu.get_barrier_semaphore()

    def greet(to):
        pl.semaphore_signal(bar, inc=1, device_id=to, device_id_type=MESH)

    for j in range(1, 8):
        greet(dev(x, (z + j) % 8 * 2 + c))
    for j in range(1, 4):
        greet(dev((x + j) % 4, r))
        greet((ctx, (tp + j) % 4))
    greet(dev(x, z * 2 + 1 - c))
    greet(((ctx + 1) % 64, tp))
    greet(((ctx + 63) % 64, tp))
    pl.semaphore_wait(bar, 16)

    partner = dev(px, r)
    core = dev(x, z * 2 + 1 - c)
    mine = kvg.at[r, pr]
    after = ((ctx + 1) % 64, tp)
    halo_x = remote(mx_.at[TOK - 16 : TOK], hx, sws.at[1], swr.at[1], after)
    halo_x.start()
    halo_bc = remote(bc_.at[TOK - 16 : TOK], hbc, sws.at[2], swr.at[2], after)
    halo_bc.start()
    kv_swap = remote(kvp.at[1 - hi], kvg.at[r, pr, hi], sws.at[0], swr.at[0], partner)
    kv_swap.start()
    q_swap = remote(q2.at[1 - hi], qb.at[hi], sws.at[3], swr.at[3], partner)
    q_swap.start()

    rows = lax.broadcasted_iota(jnp.int32, (TOK, TOK), 0)
    cols = lax.broadcasted_iota(jnp.int32, (TOK, TOK), 1)
    causal = rows >= cols
    loads[0].wait()
    loads[1].wait()
    cum = dot(causal.astype(F32), decay[...], precision=EXACT)
    eye = (lax.broadcasted_iota(jnp.int32, (32, 32), 0) == lax.broadcasted_iota(jnp.int32, (32, 32), 1)).astype(F32)
    cumt[...] = dot(eye, cum, NT, EXACT)
    stept[...] = dot(eye, step[...], NT, EXACT)
    last = cum[TOK - 1 : TOK]
    wend = jnp.exp(last - cum) * step[...]
    cum3[...] = jnp.concatenate(split3(cum), axis=1)
    loads[8].wait()
    wide = jnp.concatenate(
        [wend, jnp.exp(cum), jnp.broadcast_to(last, (8, 32)), jnp.broadcast_to(dskip[...], (8, 32))], axis=0
    )
    wide = jnp.concatenate(split3(wide), axis=1)
    for k in range(4):
        head = lax.broadcasted_iota(jnp.int32, (96, 512), 0) % 32
        lane_head = (lax.broadcasted_iota(jnp.int32, (96, 512), 1) + 512 * k) // 64
        part = dot(wide, (head == lane_head).astype(F32).astype(BF16))
        for q in range(4):
            spx[4 * k + q] = part[:, q * 128 : (q + 1) * 128]

    sends = []

    def ring(slot, d, k):
        copy = remote(slot, slot, rs.at[k], rr.at[k], dev(x, (zp if d == 0 else zm) * 2 + c))
        copy.start()
        sends.append(copy)
        return copy

    def pass_on(slot, k, s, rv, to):
        copy = remote(slot, slot, s.at[k], rv.at[k], to)
        copy.start()
        sends.append(copy)
        return copy

    core_in = {}

    def to_core(slot, k):
        core_in[k] = pass_on(slot, k, cs, cr, core)

    hops = {}
    kv_own.wait()
    kv_swap.wait()
    x_swap = remote(mine, mine, xs.at[0], xr.at[0], dev(xn, r))
    x_swap.start()
    hops[0, 0, 0] = ring(mine, 0, 0)
    hops[1, 0, 0] = ring(mine, 1, 1)
    to_core(mine, 0)

    for k in range(2, 8):
        loads[k].wait()
    halo_x.wait()
    halo_bc.wait()
    first = ctx > 0

    def conv(chunk, before, weight, bias):
        win[0:16] = jnp.where(first, before.astype(F32), 0.0)
        win[16:144] = chunk.astype(F32)
        w = weight.astype(F32)
        total = jnp.broadcast_to(bias, (TOK, 128))
        for k in range(4):
            total = total + win[13 + k : 13 + k + TOK] * w[k : k + 1]
        return silu(total).astype(BF16)

    for k in range(2):
        cut = slice(k * 128, k * 128 + 128)
        bcv[k] = conv(bc[:, cut], hbc[:, cut], wbc[:, cut], bbc[:, cut])
    btr[...] = bcv[0].astype(F32).T.astype(BF16)

    def conv_pair(p, carry):
        cut = pl.ds(pl.multiple_of(p * 128, 128), 128)
        xc[p] = conv(mx[:, cut], hx[:, cut], wx[:, cut], bx[:, cut])
        return carry

    lax.fori_loop(0, PAIRS, conv_pair, 0)

    row16 = lax.broadcasted_iota(jnp.int32, (16, 128), 0)

    def log_rows(v):
        top, mid, low = split3(jnp.broadcast_to(v, (16, 128)))
        zero = jnp.zeros((16, 128), BF16)
        return jnp.where(row16 == 0, top, jnp.where(row16 == 1, mid, jnp.where(row16 == 2, low, zero)))

    def read_log(msg_tail):
        v = msg_tail.astype(F32)
        return v[0:1] + v[1:2] + v[2:3]

    def local_state(p):
        weighted = (xc[p].astype(F32) * spx[p, 0:TOK]).astype(BF16)
        return dot(btr[...], weighted).astype(BF16), log_rows(spx[p, 256:257])

    def state_for_core(k, carry):
        state, logs = local_state(2 * k + 1 - c)
        other[k, 0:NS] = state
        other[k, NS:MSG] = logs
        return carry

    lax.fori_loop(0, 8, state_for_core, 0, unroll=4)
    core_swap = remote(other, both.at[c], ms.at[0], mr.at[0], core)
    core_swap.start()

    def state_own(k, carry):
        state, logs = local_state(2 * k + c)
        both[c, k, 0:NS] = state
        both[c, k, NS:MSG] = logs
        return carry

    lax.fori_loop(0, 8, state_own, 0, unroll=4)
    x_swap.wait()
    theirs = kvg.at[r, 1 - pr]
    hops[0, 0, 1] = ring(theirs, 0, 2)
    hops[1, 0, 1] = ring(theirs, 1, 3)
    to_core(theirs, 1)
    core_swap.wait()

    def state_copy(k):
        return remote(smsg.at[k], rmsg.at[z], a1s.at[k], a1r.at[z], dev(x, k * 2 + c))

    def chip_state(k):
        log0, log1 = read_log(both[0, k, NS:MSG]), read_log(both[1, k, NS:MSG])
        state = jnp.exp(log1) * both[0, k, 0:NS].astype(F32) + both[1, k, 0:NS].astype(F32)
        return state.astype(BF16), log_rows(log0 + log1)

    def send_state(j, carry):
        k = (z + j) % 8
        state, logs = chip_state(k)
        smsg[k, 0:NS] = state
        smsg[k, NS:MSG] = logs
        state_copy(k).start()
        return carry

    lax.fori_loop(1, 8, send_state, 0)
    state, logs = chip_state(z)
    rmsg[z, 0:NS] = state
    rmsg[z, NS:MSG] = logs

    def slot_at(zo, q):
        return kvg.at[zo % 8 * 2 + c, pr if q == 0 else 1 - pr]

    def source(d, s):
        return z + 7 - s if d == 0 else z + s + 1

    def take_ring(s):
        if s < 2:
            for q in range(2):
                for d in range(2):
                    hops[d, s, q].wait_recv()
                    slot = slot_at(source(d, s), q)
                    if s == 0 or q == 0:
                        hops[d, s + 1, q] = ring(slot, d, 4 + s * 4 + q * 2 + d)
                    to_core(slot, 2 + s * 4 + q * 2 + d)
            return
        for d in range(2):
            hops[d, s, 0].wait_recv()
            slot = slot_at(source(d, s), 0)
            if s == 2:
                hops[d, 3, 0] = ring(slot.at[d], d, 10 + d)
            else:
                slot = slot.at[d]
            side[s, d] = pass_on(slot, (s - 2) * 2 + d, fs, fr, dev(xn, r))
            to_core(slot, 10 + (s - 2) * 4 + d)

    side = {}

    def take_side(s):
        for d in range(2):
            side[s, d].wait_recv()
            slot = slot_at(source(d, s), 1)
            to_core(slot if s == 2 else slot.at[d], 12 + (s - 2) * 4 + d)

    gmat[...] = dot(bcv[1], bcv[0], NT)
    lane = lax.broadcasted_iota(jnp.int32, (TOK, 128), 1)
    col_head = lax.broadcasted_iota(jnp.int32, (96, 256), 0) % 32
    col_lane = lax.broadcasted_iota(jnp.int32, (96, 256), 1) // 128

    def one_head(h, col_log):
        gap = jnp.where(causal, col_log - cumt[pl.ds(h, 1), :], NEG)
        return (gmat[...] * jnp.exp(gap) * stept[pl.ds(h, 1), :]).astype(BF16)

    def intra(p, carry):
        h = 2 * p
        col = dot(cum3[...], (col_head == h + col_lane).astype(F32).astype(BF16))
        mixing = jnp.concatenate([one_head(h, col[:, :128]), one_head(h + 1, col[:, 128:])], axis=1)
        xp = xc[p]
        zero = jnp.zeros_like(xp)
        stacked = jnp.concatenate([jnp.where(lane < 64, xp, zero), jnp.where(lane < 64, zero, xp)], axis=0)
        lanes = pl.ds(pl.multiple_of(p * 128, 128), 128)
        g = silu(gate[:, lanes].astype(F32))
        ylocal[p] = (dot(mixing, stacked) + spx[p, 264:265] * xp.astype(F32)) * g
        egate[p] = spx[p, TOK : 2 * TOK] * g
        return carry

    loads[9].wait()
    loads[10].wait()
    lax.fori_loop(0, 6, intra, 0, unroll=2)
    take_ring(0)
    lax.fori_loop(6, 16, intra, 0, unroll=2)
    take_ring(1)

    def chain(k, carry):
        state, logs = carry

        @pl.when(k != z)
        def _():
            remote(smsg.at[k], rmsg.at[k], a1s.at[k], a1r.at[k], dev(x, k * 2 + c)).wait_recv()

        pre[k] = state
        clog[k] = jnp.broadcast_to(logs, (8, 128))
        new = read_log(rmsg[k, NS:MSG])
        return jnp.exp(new) * state + rmsg[k, 0:NS].astype(F32), logs + new

    state, logs = lax.fori_loop(0, 8, chain, (jnp.zeros((NS, 128), F32), jnp.zeros((1, 128), F32)))
    xsend[0:NS] = state.astype(BF16)
    xsend[NS:MSG] = log_rows(logs)

    def x_copy(j):
        to = (x + j) % 4
        return remote(xsend, xrecv.at[x], xxs.at[to], xxr.at[x], dev(to, r))

    for j in range(1, 4):
        x_copy(j).start()

    log_scale = math.log2(math.e) / math.sqrt(128)
    ones = jnp.ones((KT, 128), BF16)
    near, far = (7, 0, 1, 2), (6, 5, 3, 4)

    def tile(pos, pk, posk, offsets, edge):
        def load(kind):
            return jnp.concatenate(
                [kvg[pl.ds((z + o) % 8 * 2, 2), pk, posk, kind].reshape(256, 128) for o in offsets], axis=0
            )

        kt = load(0)
        vt = jnp.concatenate([load(1), ones], axis=1)
        if edge:
            lanes = lax.broadcasted_iota(jnp.int32, (1, KT), 1)
            key = jnp.zeros((1, KT), jnp.int32)
            for i, o in enumerate(offsets):
                key = jnp.where(lanes // 256 == i, (z + o) % 8 * 256 + lanes % 256, key)
        for i in range(ROWS // RC):
            cut = slice(i * RC, i * RC + RC)
            s = dot(qb[pos, cut], kt, NT)
            if edge:
                tok = (lax.broadcasted_iota(jnp.int32, (RC, KT), 0) + i * RC) // 8
                s = jnp.where(key <= tok + r * 128, s, NEG)
            old = mrun[pos, cut]
            new = jnp.maximum(old, jnp.max(s, axis=1, keepdims=True))
            p = jnp.exp2((s - jnp.concatenate([new] * (KT // 128), axis=1)) * log_scale)
            fade = jnp.exp2((old - new) * log_scale)
            acc[pos, cut] = acc[pos, cut] * jnp.concatenate([fade, fade], axis=1) + dot(p.astype(BF16), vt)
            mrun[pos, cut] = new

    def whole(pos, offsets):
        def one(kx, carry):
            pk = kx + (kx // 2) * (3 - 2 * kx)
            tile(pos, pk, kx // 2, offsets, False)
            return carry

        lax.fori_loop(0, pr + pos * (3 - 2 * pr), one, 0)

    def close(pos):
        for i in range(ROWS // RC):
            cut = slice(i * RC, i * RC + RC)
            a = acc[pos, cut]
            obuf[pos, cut] = (a[:, :128] / a[:, 128:]).astype(BF16)

    mrun[...] = jnp.full((2, ROWS, 128), NEG, F32)
    acc[...] = jnp.zeros((2, ROWS, 256), F32)
    q_swap.wait()
    q_own.wait()
    for k in (0, 1, 2, 3, 4, 5, 7, 9):
        core_in[k].wait_recv()
    tile(1 - hi, pr, 1 - hi, near, True)

    enter = jnp.zeros((NS, 128), F32)
    for j in range(4):

        @pl.when(x != j)
        def _():
            remote(xsend, xrecv.at[j], xxs.at[j], xxr.at[j], dev(j, r)).wait_recv()

    xrecv[x] = xsend[...]
    for j in range(3):
        enter = jnp.where(j < x, jnp.exp(read_log(xrecv[j, NS:MSG])) * enter + xrecv[j, 0:NS].astype(F32), enter)

    def back_copy(k):
        return remote(isend.at[k], iback.at[z], a2s.at[k], a2r.at[z], dev(x, k * 2 + c))

    def send_back(j, carry):
        k = (z + j) % 8
        isend[k] = (jnp.exp(clog[k, 0:1]) * enter + pre[k]).astype(BF16)
        back_copy(k).start()
        return carry

    lax.fori_loop(1, 8, send_back, 0)
    iback[z] = (jnp.exp(clog[z, 0:1]) * enter + pre[z]).astype(BF16)

    take_ring(2)
    whole(1 - hi, near)
    take_ring(3)
    take_side(2)
    tile(hi, pr, hi, near, True)
    take_side(3)
    whole(hi, near)

    def wait_back(j, carry):
        k = (z + j) % 8
        remote(isend.at[k], iback.at[k], a2s.at[k], a2r.at[k], dev(x, k * 2 + c)).wait_recv()
        return carry

    lax.fori_loop(1, 8, wait_back, 0)

    def hand_over(k, carry):
        before = iback[k]
        past = jnp.exp(read_log(both[0, k, NS:MSG])) * before.astype(F32) + both[0, k, 0:NS].astype(F32)
        past = past.astype(BF16)
        irecv[c, k] = jnp.where(c == 0, before, past)
        ipass[k] = jnp.where(c == 0, past, before)
        return carry

    lax.fori_loop(0, 8, hand_over, 0)
    state_swap = remote(ipass, irecv.at[c], bs.at[0], br.at[0], core)
    state_swap.start()

    for k in (6, 8) + tuple(range(10, 18)):
        core_in[k].wait_recv()
    tile(1 - hi, pr, 1 - hi, far, True)
    whole(1 - hi, far)
    close(1 - hi)
    o_swap = remote(obuf.at[1 - hi], att.at[hi], os_.at[0], or_.at[0], partner)
    o_swap.start()

    state_swap.wait()

    def finish(p, square):
        y = ylocal[p] + egate[p] * dot(bcv[1], irecv[p % 2, p // 2])
        ylocal[p] = y
        return square + y * y

    square = lax.fori_loop(0, PAIRS, finish, jnp.zeros((TOK, 128), F32), unroll=4)
    norm = lax.rsqrt(jnp.sum(square, axis=1, keepdims=True) * (1.0 / 2048) + NORM_EPS)

    def scale(p, carry):
        lanes = pl.ds(pl.multiple_of(p * 128, 128), 128)
        v = (ylocal[p] * norm * gain[:, lanes]).astype(BF16)
        for k in range(TP):
            nbuf[k, :, lanes] = v[k * 32 : k * 32 + 32]
        return carry

    lax.fori_loop(0, PAIRS, scale, 0, unroll=4)

    def row_copy(j):
        to = (tp + j) % TP
        return remote(nbuf.at[to], nrecv.at[tp], tps.at[to], tpr.at[tp], (ctx, to))

    for j in range(1, TP):
        row_copy(j).start()
    nrecv[tp] = nbuf[tp]

    tile(hi, pr, hi, far, True)
    whole(hi, far)
    close(hi)
    o_own = local(obuf.at[hi], att.at[hi], 13)
    o_own.start()

    for j in range(1, TP):
        k = (tp + j) % TP
        remote(nbuf.at[k], nrecv.at[k], tps.at[k], tpr.at[k], (ctx, k)).wait_recv()
    for k in range(TP):
        out[:, k * 2048 : (k + 1) * 2048] = nrecv[k].astype(F32)

    def left_group(j, carry):
        k = (z + j) % 8
        state_copy(k).wait_send()
        back_copy(k).wait_send()
        return carry

    lax.fori_loop(1, 8, left_group, 0)
    for j in range(1, 4):
        x_copy(j).wait_send()
        row_copy(j).wait_send()
    for copy in sends:
        copy.wait_send()
    o_own.wait()
    o_swap.wait()


def per_device(
    mamba_x, bc_in, gate_z, conv_x_weight, conv_x_bias, conv_bc_weight, conv_bc_bias,
    decay_log, step_size, d_skip, norm_gain, queries, attn_keys, attn_values,
):
    bc = bc_in.reshape(TOK, 256)
    q2 = queries.reshape(TOK, 2, 8, 128).transpose(1, 0, 2, 3).reshape(2, ROWS, 128)
    kvp = jnp.stack([attn_keys, attn_values]).transpose(2, 0, 1, 3)
    args = (
        mamba_x, bc, gate_z, conv_x_weight, conv_x_bias.reshape(1, 2048), conv_bc_weight.reshape(4, 256),
        conv_bc_bias.reshape(1, 256), decay_log, step_size, d_skip.reshape(1, 32), norm_gain.reshape(1, 2048), q2, kvp,
    )
    vmem = pl.BlockSpec(memory_space=pltpu.VMEM)
    dma = lambda *n: pltpu.SemaphoreType.DMA(n)
    buf = pltpu.VMEM
    msgs = (8, MSG, 128)
    out, att = pl.pallas_call(
        body,
        out_shape=(
            jax.ShapeDtypeStruct((32, 8192), F32),
            jax.ShapeDtypeStruct((2, ROWS, 128), BF16),
        ),
        in_specs=[pl.BlockSpec(memory_space=pl.ANY)] * 13,
        out_specs=(vmem, vmem),
        scratch_shapes=[buf(a.shape, a.dtype) for a in args[:11]]
        + [
            buf((16, 2048), BF16), buf((16, 256), BF16), buf((144, 128), F32), buf((PAIRS, TOK, 128), BF16),
            buf((2, TOK, 128), BF16), buf((NS, TOK), BF16), buf((32, TOK), F32), buf((32, TOK), F32),
            buf((TOK, 96), BF16), buf((PAIRS, 272, 128), F32), buf((TOK, TOK), F32),
            buf((PAIRS, TOK, 128), F32), buf((PAIRS, TOK, 128), F32),
            buf(msgs, BF16), buf((2,) + msgs, BF16), buf(msgs, BF16), buf(msgs, BF16),
            buf((8, NS, 128), F32), buf((8, 8, 128), F32), buf((MSG, 128), BF16), buf((4, MSG, 128), BF16),
            buf((8, NS, 128), BF16), buf((8, NS, 128), BF16), buf((8, NS, 128), BF16), buf((2, 8, NS, 128), BF16),
            buf((2, ROWS, 128), BF16), buf((16, 2, 2, 2, 128, 128), BF16), buf((2, ROWS, 256), F32),
            buf((2, ROWS, 128), F32), buf((2, ROWS, 128), BF16), buf((TP, 32, 2048), BF16), buf((TP, 32, 2048), BF16),
            dma(14), dma(4), dma(4), dma(1), dma(1), dma(12), dma(12), dma(18), dma(18), dma(4), dma(4), dma(1), dma(1),
            dma(8), dma(8), dma(4), dma(4), dma(8), dma(8), dma(1), dma(1), dma(TP), dma(TP), dma(1), dma(1),
        ],
        compiler_params=pltpu.CompilerParams(
            collective_id=0, has_side_effects=True, vmem_limit_bytes=56 << 20
        ),
    )(*args)
    attn = att.reshape(2, TOK, 8, 128).transpose(1, 0, 2, 3).reshape(TOK, 16, 128)
    return out, attn


def solution(mesh):
    in_specs = (
        P("ctx", "tp"), P("ctx", None, "tp"), P("ctx", "tp"), P(None, "tp"), P("tp"), P(None, None, "tp"),
        P(None, "tp"), P("ctx", "tp"), P("ctx", "tp"), P("tp"), P("tp"), P("ctx", "tp", None),
        P("ctx", "tp", None), P("ctx", "tp", None),
    )
    out_specs = (P(("ctx", "tp"), None), P("ctx", "tp", None))
    return jax.shard_map(per_device, mesh=mesh, in_specs=in_specs, out_specs=out_specs, check_vma=False)
```

```python
import functools
import math

import jax
import jax.numpy as jnp
from jax import lax
from jax.experimental import pallas as pl
from jax.experimental.pallas import tpu as pltpu
from jax.sharding import PartitionSpec as P

MESH = pl.DeviceIdType.MESH
F32 = jnp.float32
BF16 = jnp.bfloat16
EXACT = lax.Precision.HIGHEST

TOK = 128
NS = 128
PAIRS = 16
TP = 4
ROWS = 1024
RC = 256
NEG = -1e30
NORM_EPS = 1e-05
MSG = 144

NT = (((1,), (1,)), ((), ()))


def dot(a, b, dims=(((1,), (0,)), ((), ())), precision=None):
    return lax.dot_general(a, b, dims, precision=precision, preferred_element_type=F32)


def silu(v):
    return v * jax.nn.sigmoid(v)


def split3(v):
    top = v.astype(BF16)
    rest = v - top.astype(F32)
    mid = rest.astype(BF16)
    low = (rest - mid.astype(F32)).astype(BF16)
    return top, mid, low


def body(
    mx_, bc_, gate_, wx_, bx_, wbc_, bbc_, decay_, step_, dskip_, gain_, q_, k_, v_,
    out, att,
    mx, bc, gate, wx, bx, wbc, bbc, decay, step, dskip, gain, q, kin, vin, q2, kvp,
    hx, hbc, win, xc, bcv, btr, cumt, cum3, spx, gmat, ylocal, egate,
    other, both, smsg, rmsg, pre, clog, xsend, xrecv, isend, iback, ipass, irecv,
    qb, kvg, acc, mrun, obuf, nbuf, nrecv,
    loc, sws, swr, xs, xr, rs, rr, cs, cr, fs, fr, ms, mr, a1s, a1r, xxs, xxr, a2s, a2r, bs, br, tps, tpr, os_, or_,
):
    ctx, tp = lax.axis_index("ctx"), lax.axis_index("tp")
    x, r = ctx // 16, ctx % 16
    z, c = r // 2, r % 2
    hi = x // 2
    px = 3 - x
    pr = x + hi * (3 - 2 * x)
    xn = x + 1 - 2 * (x % 2)
    zp, zm = (z + 1) % 8, (z + 7) % 8

    def dev(x_, r_):
        return (x_ * 16 + r_, tp)

    def remote(src, dst, s, rv, to):
        return pltpu.make_async_remote_copy(
            src_ref=src, dst_ref=dst, send_sem=s, recv_sem=rv, device_id=to, device_id_type=MESH
        )

    def local(src, dst, k):
        return pltpu.make_async_copy(src, dst, loc.at[k])

    bar = pltpu.get_barrier_semaphore()

    def greet(to):
        pl.semaphore_signal(bar, inc=1, device_id=to, device_id_type=MESH)

    for j in range(1, 8):
        greet(dev(x, (z + j) % 8 * 2 + c))
    for j in range(1, 4):
        greet(dev((x + j) % 4, r))
        greet((ctx, (tp + j) % 4))
    greet(dev(x, z * 2 + 1 - c))
    greet(((ctx + 1) % 64, tp))
    greet(((ctx + 63) % 64, tp))

    brought = (
        (k_, kin), (v_, vin), (decay_, decay), (step_, step), (dskip_, dskip), (q_, q), (bc_, bc), (mx_, mx), (wx_, wx),
        (bx_, bx), (wbc_, wbc), (bbc_, bbc), (gate_, gate), (gain_, gain),
    )
    loads = [local(a, b, k) for k, (a, b) in enumerate(brought)]
    for load in loads:
        load.start()
    loads[0].wait()
    loads[1].wait()
    for k, part in enumerate((kin, vin)):
        part = part[...].astype(F32)
        for j in range(2):
            kvp[j, k] = part[:, j].astype(BF16)
    kv_own = local(kvp.at[hi], kvg.at[r, pr, hi], 14)
    kv_own.start()
    pl.semaphore_wait(bar, 16)

    partner = dev(px, r)
    core = dev(x, z * 2 + 1 - c)
    mine = kvg.at[r, pr]
    after = ((ctx + 1) % 64, tp)
    halo_x = remote(mx_.at[TOK - 16 : TOK], hx, sws.at[1], swr.at[1], after)
    halo_x.start()
    halo_bc = remote(bc_.at[TOK - 16 : TOK], hbc, sws.at[2], swr.at[2], after)
    halo_bc.start()
    kv_swap = remote(kvp.at[1 - hi], kvg.at[r, pr, hi], sws.at[0], swr.at[0], partner)
    kv_swap.start()
    loads[5].wait()
    heads = q[...].astype(F32)
    for j in range(2):
        q2[j] = heads[:, 8 * j : 8 * j + 8].reshape(ROWS, 128).astype(BF16)
    q_own = local(q2.at[hi], qb.at[hi], 15)
    q_own.start()
    q_swap = remote(q2.at[1 - hi], qb.at[hi], sws.at[3], swr.at[3], partner)
    q_swap.start()

    rows = lax.broadcasted_iota(jnp.int32, (TOK, TOK), 0)
    cols = lax.broadcasted_iota(jnp.int32, (TOK, TOK), 1)
    causal = rows >= cols
    loads[2].wait()
    loads[3].wait()
    tril = causal.astype(F32)
    cum = dot(tril, decay[...], NT, EXACT)
    cumt[...] = dot(decay[...], tril, NT, EXACT)
    last = cum[TOK - 1 : TOK]
    wend = jnp.exp(last - cum) * dot((rows == cols).astype(F32), step[...], NT, EXACT)
    cum3[...] = jnp.concatenate(split3(cum), axis=1)
    loads[4].wait()
    wide = jnp.concatenate(
        [wend, jnp.exp(cum), jnp.broadcast_to(last, (8, 32)), jnp.broadcast_to(dskip[...], (8, 32))], axis=0
    )
    wide = jnp.concatenate(split3(wide), axis=1)
    for k in range(4):
        head = lax.broadcasted_iota(jnp.int32, (96, 512), 0) % 32
        lane_head = (lax.broadcasted_iota(jnp.int32, (96, 512), 1) + 512 * k) // 64
        part = dot(wide, (head == lane_head).astype(F32).astype(BF16))
        for j in range(4):
            spx[4 * k + j] = part[:, j * 128 : (j + 1) * 128]

    sends = []

    def ring(slot, d, k):
        copy = remote(slot, slot, rs.at[k], rr.at[k], dev(x, (zp if d == 0 else zm) * 2 + c))
        copy.start()
        sends.append(copy)
        return copy

    def pass_on(slot, k, s, rv, to):
        copy = remote(slot, slot, s.at[k], rv.at[k], to)
        copy.start()
        sends.append(copy)
        return copy

    core_in = {}

    def to_core(slot, k):
        core_in[k] = pass_on(slot, k, cs, cr, core)

    hops = {}
    kv_own.wait()
    kv_swap.wait()
    x_swap = remote(mine, mine, xs.at[0], xr.at[0], dev(xn, r))
    x_swap.start()
    hops[0, 0, 0] = ring(mine, 0, 0)
    hops[1, 0, 0] = ring(mine, 1, 1)
    to_core(mine, 0)

    for k in range(6, 12):
        loads[k].wait()
    halo_x.wait()
    halo_bc.wait()
    first = ctx > 0

    def conv(chunk, before, weight, bias):
        win[0:16] = jnp.where(first, before.astype(F32), 0.0)
        win[16:144] = chunk.astype(F32)
        w = weight.astype(F32)
        total = jnp.broadcast_to(bias, (TOK, 128))
        for k in range(4):
            total = total + win[13 + k : 13 + k + TOK] * w[k : k + 1]
        return silu(total).astype(BF16)

    for k in range(2):
        bcv[k] = conv(
            bc[...].astype(F32)[:, k], hbc[...].astype(F32)[:, k], wbc[...].astype(F32)[:, k], bbc[k : k + 1]
        )
    btr[...] = bcv[0].astype(F32).T.astype(BF16)

    def conv_pair(p, carry):
        cut = pl.ds(pl.multiple_of(p * 128, 128), 128)
        xc[p] = conv(mx[:, cut], hx[:, cut], wx[:, cut], bx[:, cut])
        return carry

    lax.fori_loop(0, PAIRS, conv_pair, 0)

    row16 = lax.broadcasted_iota(jnp.int32, (16, 128), 0)

    def log_rows(v):
        top, mid, low = split3(jnp.broadcast_to(v, (16, 128)))
        zero = jnp.zeros((16, 128), BF16)
        return jnp.where(row16 == 0, top, jnp.where(row16 == 1, mid, jnp.where(row16 == 2, low, zero)))

    def read_log(msg_tail):
        v = msg_tail.astype(F32)
        return v[0:1] + v[1:2] + v[2:3]

    def local_state(p):
        weighted = (xc[p].astype(F32) * spx[p, 0:TOK]).astype(BF16)
        return dot(btr[...], weighted).astype(BF16), log_rows(spx[p, 256:257])

    def state_for_core(k, carry):
        state, logs = local_state(2 * k + 1 - c)
        other[k, 0:NS] = state
        other[k, NS:MSG] = logs
        return carry

    lax.fori_loop(0, 8, state_for_core, 0, unroll=4)
    core_swap = remote(other, both.at[c], ms.at[0], mr.at[0], core)
    core_swap.start()

    def state_own(k, carry):
        state, logs = local_state(2 * k + c)
        both[c, k, 0:NS] = state
        both[c, k, NS:MSG] = logs
        return carry

    lax.fori_loop(0, 8, state_own, 0, unroll=4)
    x_swap.wait()
    theirs = kvg.at[r, 1 - pr]
    hops[0, 0, 1] = ring(theirs, 0, 2)
    hops[1, 0, 1] = ring(theirs, 1, 3)
    to_core(theirs, 1)
    core_swap.wait()

    def state_copy(k):
        return remote(smsg.at[k], rmsg.at[z], a1s.at[k], a1r.at[z], dev(x, k * 2 + c))

    def chip_state(k):
        log0, log1 = read_log(both[0, k, NS:MSG]), read_log(both[1, k, NS:MSG])
        state = jnp.exp(log1) * both[0, k, 0:NS].astype(F32) + both[1, k, 0:NS].astype(F32)
        return state.astype(BF16), log_rows(log0 + log1)

    def send_state(j, carry):
        k = (z + j) % 8
        state, logs = chip_state(k)
        smsg[k, 0:NS] = state
        smsg[k, NS:MSG] = logs
        state_copy(k).start()
        return carry

    lax.fori_loop(1, 8, send_state, 0)
    state, logs = chip_state(z)
    rmsg[z, 0:NS] = state
    rmsg[z, NS:MSG] = logs

    def slot_at(zo, q):
        return kvg.at[zo % 8 * 2 + c, pr if q == 0 else 1 - pr]

    def source(d, s):
        return z + 7 - s if d == 0 else z + s + 1

    def take_ring(s):
        if s < 2:
            for q in range(2):
                for d in range(2):
                    hops[d, s, q].wait_recv()
                    slot = slot_at(source(d, s), q)
                    if s == 0 or q == 0:
                        hops[d, s + 1, q] = ring(slot, d, 4 + s * 4 + q * 2 + d)
                    to_core(slot, 2 + s * 4 + q * 2 + d)
            return
        for d in range(2):
            hops[d, s, 0].wait_recv()
            slot = slot_at(source(d, s), 0)
            if s == 2:
                hops[d, 3, 0] = ring(slot.at[d], d, 10 + d)
            else:
                slot = slot.at[d]
            side[s, d] = pass_on(slot, (s - 2) * 2 + d, fs, fr, dev(xn, r))
            to_core(slot, 10 + (s - 2) * 4 + d)

    side = {}

    def take_side(s):
        for d in range(2):
            side[s, d].wait_recv()
            slot = slot_at(source(d, s), 1)
            to_core(slot if s == 2 else slot.at[d], 12 + (s - 2) * 4 + d)

    gmat[...] = dot(bcv[1], bcv[0], NT)
    lane = lax.broadcasted_iota(jnp.int32, (TOK, 128), 1)
    col_head = lax.broadcasted_iota(jnp.int32, (96, 256), 0) % 32
    col_lane = lax.broadcasted_iota(jnp.int32, (96, 256), 1) // 128

    def one_head(h, col_log):
        gap = jnp.where(causal, col_log - cumt[pl.ds(h, 1), :], NEG)
        return (gmat[...] * jnp.exp(gap) * step[pl.ds(h, 1), :]).astype(BF16)

    def intra(p, carry):
        h = 2 * p
        col = dot(cum3[...], (col_head == h + col_lane).astype(F32).astype(BF16))
        mixing = jnp.concatenate([one_head(h, col[:, :128]), one_head(h + 1, col[:, 128:])], axis=1)
        xp = xc[p]
        zero = jnp.zeros_like(xp)
        stacked = jnp.concatenate([jnp.where(lane < 64, xp, zero), jnp.where(lane < 64, zero, xp)], axis=0)
        lanes = pl.ds(pl.multiple_of(p * 128, 128), 128)
        g = silu(gate[:, lanes].astype(F32))
        ylocal[p] = (dot(mixing, stacked) + spx[p, 264:265] * xp.astype(F32)) * g
        egate[p] = spx[p, TOK : 2 * TOK] * g
        return carry

    loads[12].wait()
    loads[13].wait()
    lax.fori_loop(0, 8, intra, 0, unroll=2)
    take_ring(0)
    lax.fori_loop(8, 16, intra, 0, unroll=2)

    log_scale = math.log2(math.e) / math.sqrt(128)
    rounds = ((0, 1, 7), (2, 6), (3, 5, 4))

    def tile(pos, kinds, offsets, edge):
        width = 256 * len(offsets)
        total = width * len(kinds)

        def load(kind):
            return jnp.concatenate(
                [
                    kvg[pl.ds((z + o) % 8 * 2, 2), pk, posk, kind].reshape(256, 128)
                    for pk, posk in kinds
                    for o in offsets
                ],
                axis=0,
            )

        kt = load(0)
        vt = jnp.concatenate([load(1), jnp.ones((total, 128), BF16)], axis=1)
        if edge:
            lanes = lax.broadcasted_iota(jnp.int32, (1, total), 1)
            key = jnp.full((1, total), -1, jnp.int32)
            for i, o in enumerate(offsets):
                here = (lanes // 256 == i + (total - width) // 256)
                key = jnp.where(here, (z + o) % 8 * 256 + lanes % 256, key)

        def scores(i):
            return dot(qb[pos, i * RC : i * RC + RC], kt, NT)

        ahead = scores(0)
        for i in range(ROWS // RC):
            cut = slice(i * RC, i * RC + RC)
            s = ahead
            if i + 1 < ROWS // RC:
                ahead = scores(i + 1)
            if edge:
                tok = (lax.broadcasted_iota(jnp.int32, (RC, total), 0) + i * RC) // 8
                s = jnp.where(key <= tok + r * 128, s, NEG)
            old = mrun[pos, cut]
            new = jnp.maximum(old, jnp.max(s, axis=1, keepdims=True))
            p = jnp.exp2((s - jnp.concatenate([new] * (total // 128), axis=1)) * log_scale)
            fade = jnp.exp2((old - new) * log_scale)
            acc[pos, cut] = acc[pos, cut] * jnp.concatenate([fade, fade], axis=1) + dot(p.astype(BF16), vt)
            mrun[pos, cut] = new

    def part_a(n):
        tile(1, ((0, 0), (1, 0)), rounds[n], False)

    def part_b(n):
        tile(1 - pr, ((1 - pr, 1 - pr), (pr, 1 - pr)), rounds[n], True)

    def part_c(n):
        tile(pr, ((pr, pr),), rounds[n], True)

    def close(pos):
        for i in range(ROWS // RC):
            cut = slice(i * RC, i * RC + RC)
            a = acc[pos, cut]
            obuf[pos, cut] = (a[:, :128] / a[:, 128:]).astype(BF16)

    mrun[...] = jnp.full((2, ROWS, 128), NEG, F32)
    acc[...] = jnp.zeros((2, ROWS, 256), F32)
    q_swap.wait()
    q_own.wait()
    for k in range(6):
        core_in[k].wait_recv()
    part_a(0)
    take_ring(1)

    def chain(k, carry):
        state, logs = carry

        @pl.when(k != z)
        def _():
            remote(smsg.at[k], rmsg.at[k], a1s.at[k], a1r.at[k], dev(x, k * 2 + c)).wait_recv()

        pre[k] = state
        clog[k] = jnp.broadcast_to(logs, (8, 128))
        new = read_log(rmsg[k, NS:MSG])
        return jnp.exp(new) * state + rmsg[k, 0:NS].astype(F32), logs + new

    state, logs = lax.fori_loop(0, 8, chain, (jnp.zeros((NS, 128), F32), jnp.zeros((1, 128), F32)))
    xsend[0:NS] = state
    xsend[NS : NS + 8] = jnp.broadcast_to(logs, (8, 128))

    def x_copy(j):
        to = (x + j) % 4
        return remote(xsend, xrecv.at[x], xxs.at[to], xxr.at[x], dev(to, r))

    for j in range(1, 4):
        x_copy(j).start()

    part_b(0)
    enter = jnp.zeros((NS, 128), F32)
    for j in range(4):

        @pl.when(x != j)
        def _():
            remote(xsend, xrecv.at[j], xxs.at[j], xxr.at[j], dev(j, r)).wait_recv()

    xrecv[x] = xsend[...]
    for j in range(3):
        enter = jnp.where(j < x, jnp.exp(xrecv[j, NS : NS + 1]) * enter + xrecv[j, 0:NS], enter)

    def back_copy(k):
        return remote(isend.at[k], iback.at[z], a2s.at[k], a2r.at[z], dev(x, k * 2 + c))

    def send_back(j, carry):
        k = (z + j) % 8
        isend[k] = jnp.exp(clog[k, 0:1]) * enter + pre[k]
        back_copy(k).start()
        return carry

    lax.fori_loop(1, 8, send_back, 0)
    iback[z] = jnp.exp(clog[z, 0:1]) * enter + pre[z]

    take_ring(2)
    part_c(0)
    for k in range(6, 10):
        core_in[k].wait_recv()
    part_a(1)
    take_ring(3)
    take_side(2)
    part_b(1)
    take_side(3)
    part_c(1)

    def wait_back(j, carry):
        k = (z + j) % 8
        remote(isend.at[k], iback.at[k], a2s.at[k], a2r.at[k], dev(x, k * 2 + c)).wait_recv()
        return carry

    lax.fori_loop(1, 8, wait_back, 0)

    def hand_over(k, carry):
        before = iback[k]
        past = jnp.exp(read_log(both[0, k, NS:MSG])) * before + both[0, k, 0:NS].astype(F32)
        irecv[c, k] = jnp.where(c == 0, before, past)
        ipass[k] = jnp.where(c == 0, past, before)
        return carry

    lax.fori_loop(0, 8, hand_over, 0)
    state_swap = remote(ipass, irecv.at[c], bs.at[0], br.at[0], core)
    state_swap.start()

    for k in range(10, 18):
        core_in[k].wait_recv()

    o_swap = remote(obuf.at[1 - hi], att.at[hi], os_.at[0], or_.at[0], partner)

    def row_copy(j):
        to = (tp + j) % TP
        return remote(nbuf.at[to], nrecv.at[tp], tps.at[to], tpr.at[tp], (ctx, to))

    def finish_all():
        state_swap.wait()

        def finish(p, square):
            state = irecv[p % 2, p // 2]
            top = state.astype(BF16)
            low = (state - top.astype(F32)).astype(BF16)
            y = ylocal[p] + egate[p] * dot(twice, jnp.concatenate([top, low], axis=0))
            ylocal[p] = y
            return square + y * y

        twice = jnp.concatenate([bcv[1], bcv[1]], axis=1)
        square = lax.fori_loop(0, PAIRS, finish, jnp.zeros((TOK, 128), F32), unroll=4)
        norm = lax.rsqrt(jnp.sum(square, axis=1, keepdims=True) * (1.0 / 2048) + NORM_EPS)

        def scale(p, carry):
            lanes = pl.ds(pl.multiple_of(p * 128, 128), 128)
            v = (ylocal[p] * norm * gain[:, lanes]).astype(BF16)
            for k in range(TP):
                nbuf[k, :, lanes] = v[k * 32 : k * 32 + 32]
            return carry

        lax.fori_loop(0, PAIRS, scale, 0, unroll=4)

        for j in range(1, TP):
            row_copy(j).start()
        nrecv[tp] = nbuf[tp]

    def last_round(it, carry):
        is_a = it == hi
        other1 = jnp.where(hi == 0, it == 1, it == 2)
        other0 = jnp.where(hi == 0, it == 2, it == 0)
        is_b = jnp.where(pr == 0, other1, other0)
        is_c = jnp.where(pr == 0, other0, other1)

        @pl.when(it == 1)
        def _():
            finish_all()

        @pl.when(is_a)
        def _():
            part_a(2)

        @pl.when(is_b)
        def _():
            part_b(2)

        @pl.when(is_c)
        def _():
            part_c(2)

        @pl.when(it == 1 - hi)
        def _():
            close(1 - hi)
            o_swap.start()

        return carry

    lax.fori_loop(0, 3, last_round, 0)
    close(hi)
    o_own = local(obuf.at[hi], att.at[hi], 16)
    o_own.start()

    for j in range(1, TP):
        k = (tp + j) % TP
        remote(nbuf.at[k], nrecv.at[k], tps.at[k], tpr.at[k], (ctx, k)).wait_recv()
    for k in range(TP):
        out[:, k * 2048 : (k + 1) * 2048] = nrecv[k].astype(F32)

    def left_group(j, carry):
        k = (z + j) % 8
        state_copy(k).wait_send()
        back_copy(k).wait_send()
        return carry

    lax.fori_loop(1, 8, left_group, 0)
    for j in range(1, 4):
        x_copy(j).wait_send()
        row_copy(j).wait_send()
    for copy in sends:
        copy.wait_send()
    o_own.wait()
    o_swap.wait()


def per_device(
    mamba_x, bc_in, gate_z, conv_x_weight, conv_x_bias, conv_bc_weight, conv_bc_bias,
    decay_log, step_size, d_skip, norm_gain, queries, attn_keys, attn_values,
):
    args = (
        mamba_x, bc_in, gate_z, conv_x_weight, conv_x_bias.reshape(1, 2048), conv_bc_weight, conv_bc_bias,
        decay_log.T, step_size.T, d_skip.reshape(1, 32), norm_gain.reshape(1, 2048), queries, attn_keys, attn_values,
    )
    vmem = pl.BlockSpec(memory_space=pltpu.VMEM)
    dma = lambda *n: pltpu.SemaphoreType.DMA(n)
    buf = pltpu.VMEM
    msgs = (8, MSG, 128)
    out, att = pl.pallas_call(
        body,
        out_shape=(
            jax.ShapeDtypeStruct((32, 8192), F32),
            jax.ShapeDtypeStruct((2, ROWS, 128), BF16),
        ),
        in_specs=[pl.BlockSpec(memory_space=pltpu.HBM)] * 14,
        out_specs=(vmem, vmem),
        scratch_shapes=[buf(a.shape, a.dtype) for a in args]
        + [
            buf((2, ROWS, 128), BF16), buf((2, 2, TOK, 128), BF16),
            buf((16, 2048), BF16), buf((16, 2, 128), BF16), buf((144, 128), F32), buf((PAIRS, TOK, 128), BF16),
            buf((2, TOK, 128), BF16), buf((NS, TOK), BF16), buf((32, TOK), F32),
            buf((TOK, 96), BF16), buf((PAIRS, 272, 128), F32), buf((TOK, TOK), F32),
            buf((PAIRS, TOK, 128), F32), buf((PAIRS, TOK, 128), F32),
            buf(msgs, BF16), buf((2,) + msgs, BF16), buf(msgs, BF16), buf(msgs, BF16),
            buf((8, NS, 128), F32), buf((8, 8, 128), F32), buf((NS + 8, 128), F32), buf((4, NS + 8, 128), F32),
            buf((8, NS, 128), F32), buf((8, NS, 128), F32), buf((8, NS, 128), F32), buf((2, 8, NS, 128), F32),
            buf((2, ROWS, 128), BF16), buf((16, 2, 2, 2, 128, 128), BF16), buf((2, ROWS, 256), F32),
            buf((2, ROWS, 128), F32), buf((2, ROWS, 128), BF16), buf((TP, 32, 2048), BF16), buf((TP, 32, 2048), BF16),
            dma(17), dma(4), dma(4), dma(1), dma(1), dma(12), dma(12), dma(18), dma(18), dma(4), dma(4), dma(1), dma(1),
            dma(8), dma(8), dma(4), dma(4), dma(8), dma(8), dma(1), dma(1), dma(TP), dma(TP), dma(1), dma(1),
        ],
        compiler_params=pltpu.CompilerParams(
            collective_id=0, has_side_effects=True, vmem_limit_bytes=60 << 20
        ),
    )(*args)
    attn = att.reshape(2, TOK, 8, 128).transpose(1, 0, 2, 3).reshape(TOK, 16, 128)
    return out, attn


def solution(mesh):
    in_specs = (
        P("ctx", "tp"), P("ctx", None, "tp"), P("ctx", "tp"), P(None, "tp"), P("tp"), P(None, None, "tp"),
        P(None, "tp"), P("ctx", "tp"), P("ctx", "tp"), P("tp"), P("tp"), P("ctx", "tp", None),
        P("ctx", "tp", None), P("ctx", "tp", None),
    )
    out_specs = (P(("ctx", "tp"), None), P("ctx", "tp", None))
    return jax.shard_map(per_device, mesh=mesh, in_specs=in_specs, out_specs=out_specs, check_vma=False)
```

```python
import functools
import math

import jax
import jax.numpy as jnp
from jax import lax
from jax.experimental import pallas as pl
from jax.experimental.pallas import tpu as pltpu
from jax.sharding import PartitionSpec as P

MESH = pl.DeviceIdType.MESH
F32 = jnp.float32
BF16 = jnp.bfloat16
EXACT = lax.Precision.HIGHEST

TOK = 128
NS = 128
PAIRS = 16
TP = 4
ROWS = 1024
RC = 256
NEG = -1e30
NORM_EPS = 1e-05
MSG = 144

NT = (((1,), (1,)), ((), ()))


def dot(a, b, dims=(((1,), (0,)), ((), ())), precision=None):
    return lax.dot_general(a, b, dims, precision=precision, preferred_element_type=F32)


def silu(v):
    return v * jax.nn.sigmoid(v)


def split3(v):
    top = v.astype(BF16)
    rest = v - top.astype(F32)
    mid = rest.astype(BF16)
    low = (rest - mid.astype(F32)).astype(BF16)
    return top, mid, low


def body(
    mx_, bc_, gate_, wx_, bx_, wbc_, bbc_, decay_, step_, dskip_, gain_, q_, k_, v_,
    out, att,
    mx, bc, gate, wx, bx, wbc, bbc, decay, step, dskip, gain, q, kin, vin, q2, kvp,
    hx, hbc, win, xc, bcv, btr, cumt, cum3, spx, gmat, ylocal, egate,
    other, both, smsg, rmsg, pre, clog, xsend, xrecv, isend, iback, ipass, irecv,
    qb, kvg, acc, mrun, obuf, oin, nbuf, nrecv,
    loc, sws, swr, xs, xr, rs, rr, cs, cr, fs, fr, ms, mr, a1s, a1r, xxs, xxr, a2s, a2r, bs, br, tps, tpr, os_, or_,
):
    ctx, tp = lax.axis_index("ctx"), lax.axis_index("tp")
    x, r = ctx // 16, ctx % 16
    z, c = r // 2, r % 2
    hi = x // 2
    px = 3 - x
    pr = x + hi * (3 - 2 * x)
    xn = x + 1 - 2 * (x % 2)
    zp, zm = (z + 1) % 8, (z + 7) % 8

    def dev(x_, r_):
        return (x_ * 16 + r_, tp)

    def remote(src, dst, s, rv, to):
        return pltpu.make_async_remote_copy(
            src_ref=src, dst_ref=dst, send_sem=s, recv_sem=rv, device_id=to, device_id_type=MESH
        )

    def local(src, dst, k):
        return pltpu.make_async_copy(src, dst, loc.at[k])

    bar = pltpu.get_barrier_semaphore()

    def greet(to):
        pl.semaphore_signal(bar, inc=1, device_id=to, device_id_type=MESH)

    for j in range(1, 8):
        greet(dev(x, (z + j) % 8 * 2 + c))
    for j in range(1, 4):
        greet(dev((x + j) % 4, r))
        greet((ctx, (tp + j) % 4))
    greet(dev(x, z * 2 + 1 - c))
    greet(((ctx + 1) % 64, tp))
    greet(((ctx + 63) % 64, tp))

    brought = (
        (k_, kin), (v_, vin), (decay_, decay), (step_, step), (dskip_, dskip), (q_, q), (bc_, bc), (mx_, mx), (wx_, wx),
        (bx_, bx), (wbc_, wbc), (bbc_, bbc), (gate_, gate), (gain_, gain),
    )
    loads = [local(a, b, k) for k, (a, b) in enumerate(brought)]
    for load in loads:
        load.start()
    loads[0].wait()
    loads[1].wait()
    for k, part in enumerate((kin, vin)):
        part = part[...].astype(F32)
        for j in range(2):
            kvp[j, k] = part[:, j].astype(BF16)
    kv_own = local(kvp.at[hi], kvg.at[r, pr, hi], 14)
    kv_own.start()
    pl.semaphore_wait(bar, 16)

    partner = dev(px, r)
    core = dev(x, z * 2 + 1 - c)
    mine = kvg.at[r, pr]
    after = ((ctx + 1) % 64, tp)
    halo_x = remote(mx_.at[TOK - 16 : TOK], hx, sws.at[1], swr.at[1], after)
    halo_x.start()
    halo_bc = remote(bc_.at[TOK - 16 : TOK], hbc, sws.at[2], swr.at[2], after)
    halo_bc.start()
    kv_swap = remote(kvp.at[1 - hi], kvg.at[r, pr, hi], sws.at[0], swr.at[0], partner)
    kv_swap.start()
    loads[5].wait()
    heads = q[...].astype(F32)
    for j in range(2):
        q2[j] = heads[:, 8 * j : 8 * j + 8].reshape(ROWS, 128).astype(BF16)
    q_own = local(q2.at[hi], qb.at[hi], 15)
    q_own.start()
    q_swap = remote(q2.at[1 - hi], qb.at[hi], sws.at[3], swr.at[3], partner)
    q_swap.start()

    rows = lax.broadcasted_iota(jnp.int32, (TOK, TOK), 0)
    cols = lax.broadcasted_iota(jnp.int32, (TOK, TOK), 1)
    causal = rows >= cols
    loads[2].wait()
    loads[3].wait()
    tril = causal.astype(F32)
    cum = dot(tril, decay[...], NT, EXACT)
    cumt[...] = dot(decay[...], tril, NT, EXACT)
    last = cum[TOK - 1 : TOK]
    wend = jnp.exp(last - cum) * dot((rows == cols).astype(F32), step[...], NT, EXACT)
    cum3[...] = jnp.concatenate(split3(cum), axis=1)
    loads[4].wait()
    wide = jnp.concatenate(
        [wend, jnp.exp(cum), jnp.broadcast_to(last, (8, 32)), jnp.broadcast_to(dskip[...], (8, 32))], axis=0
    )
    wide = jnp.concatenate(split3(wide), axis=1)
    for k in range(4):
        head = lax.broadcasted_iota(jnp.int32, (96, 512), 0) % 32
        lane_head = (lax.broadcasted_iota(jnp.int32, (96, 512), 1) + 512 * k) // 64
        part = dot(wide, (head == lane_head).astype(F32).astype(BF16))
        for j in range(4):
            spx[4 * k + j] = part[:, j * 128 : (j + 1) * 128]

    sends = []

    def ring(slot, d, k):
        copy = remote(slot, slot, rs.at[k], rr.at[k], dev(x, (zp if d == 0 else zm) * 2 + c))
        copy.start()
        sends.append(copy)
        return copy

    def pass_on(slot, k, s, rv, to):
        copy = remote(slot, slot, s.at[k], rv.at[k], to)
        copy.start()
        sends.append(copy)
        return copy

    core_in = {}

    def to_core(slot, k):
        core_in[k] = pass_on(slot, k, cs, cr, core)

    hops = {}
    kv_own.wait()
    kv_swap.wait()
    x_swap = remote(mine, mine, xs.at[0], xr.at[0], dev(xn, r))
    x_swap.start()
    hops[0, 0, 0] = ring(mine, 0, 0)
    hops[1, 0, 0] = ring(mine, 1, 1)
    to_core(mine, 0)

    for k in range(6, 12):
        loads[k].wait()
    halo_x.wait()
    halo_bc.wait()
    first = ctx > 0

    def conv(chunk, before, weight, bias):
        win[0:16] = jnp.where(first, before.astype(F32), 0.0)
        win[16:144] = chunk.astype(F32)
        w = weight.astype(F32)
        total = jnp.broadcast_to(bias, (TOK, 128))
        for k in range(4):
            total = total + win[13 + k : 13 + k + TOK] * w[k : k + 1]
        return silu(total).astype(BF16)

    for k in range(2):
        bcv[k] = conv(
            bc[...].astype(F32)[:, k], hbc[...].astype(F32)[:, k], wbc[...].astype(F32)[:, k], bbc[k : k + 1]
        )
    btr[...] = bcv[0].astype(F32).T.astype(BF16)

    def conv_pair(p, carry):
        cut = pl.ds(pl.multiple_of(p * 128, 128), 128)
        xc[p] = conv(mx[:, cut], hx[:, cut], wx[:, cut], bx[:, cut])
        return carry

    lax.fori_loop(0, PAIRS, conv_pair, 0)

    row16 = lax.broadcasted_iota(jnp.int32, (16, 128), 0)

    def log_rows(v):
        top, mid, low = split3(jnp.broadcast_to(v, (16, 128)))
        zero = jnp.zeros((16, 128), BF16)
        return jnp.where(row16 == 0, top, jnp.where(row16 == 1, mid, jnp.where(row16 == 2, low, zero)))

    def read_log(msg_tail):
        v = msg_tail.astype(F32)
        return v[0:1] + v[1:2] + v[2:3]

    def local_state(p):
        weighted = (xc[p].astype(F32) * spx[p, 0:TOK]).astype(BF16)
        return dot(btr[...], weighted).astype(BF16), log_rows(spx[p, 256:257])

    def state_for_core(k, carry):
        state, logs = local_state(2 * k + 1 - c)
        other[k, 0:NS] = state
        other[k, NS:MSG] = logs
        return carry

    lax.fori_loop(0, 8, state_for_core, 0, unroll=4)
    core_swap = remote(other, both.at[c], ms.at[0], mr.at[0], core)
    core_swap.start()
    x_swap.wait()
    theirs = kvg.at[r, 1 - pr]
    hops[0, 0, 1] = ring(theirs, 0, 2)
    hops[1, 0, 1] = ring(theirs, 1, 3)
    to_core(theirs, 1)

    def state_own(k, carry):
        state, logs = local_state(2 * k + c)
        both[c, k, 0:NS] = state
        both[c, k, NS:MSG] = logs
        return carry

    lax.fori_loop(0, 8, state_own, 0, unroll=4)
    core_swap.wait()

    def state_copy(k):
        return remote(smsg.at[k], rmsg.at[z], a1s.at[k], a1r.at[z], dev(x, k * 2 + c))

    def chip_state(k):
        log0, log1 = read_log(both[0, k, NS:MSG]), read_log(both[1, k, NS:MSG])
        state = jnp.exp(log1) * both[0, k, 0:NS].astype(F32) + both[1, k, 0:NS].astype(F32)
        return state.astype(BF16), log_rows(log0 + log1)

    def send_state(j, carry):
        k = (z + j) % 8
        state, logs = chip_state(k)
        smsg[k, 0:NS] = state
        smsg[k, NS:MSG] = logs
        state_copy(k).start()
        return carry

    lax.fori_loop(1, 8, send_state, 0)
    state, logs = chip_state(z)
    rmsg[z, 0:NS] = state
    rmsg[z, NS:MSG] = logs

    def slot_at(zo, q):
        return kvg.at[zo % 8 * 2 + c, pr if q == 0 else 1 - pr]

    def source(d, s):
        return z + 7 - s if d == 0 else z + s + 1

    def take(s, q):
        for d in range(2):
            hops[d, s, q].wait_recv()
            slot = slot_at(source(d, s), q)
            if s == 0 or q == 0:
                hops[d, s + 1, q] = ring(slot, d, 4 + s * 4 + q * 2 + d)
            to_core(slot, 2 + s * 4 + q * 2 + d)

    def take_ring(s):
        for d in range(2):
            hops[d, s, 0].wait_recv()
            slot = slot_at(source(d, s), 0)
            if s == 2:
                hops[d, 3, 0] = ring(slot.at[d], d, 10 + d)
            else:
                slot = slot.at[d]
            side[s, d] = pass_on(slot, (s - 2) * 2 + d, fs, fr, dev(xn, r))
            to_core(slot, 10 + (s - 2) * 4 + d)

    side = {}

    def take_side(s):
        for d in range(2):
            side[s, d].wait_recv()
            slot = slot_at(source(d, s), 1)
            to_core(slot if s == 2 else slot.at[d], 12 + (s - 2) * 4 + d)

    gmat[...] = dot(bcv[1], bcv[0], NT)
    lane = lax.broadcasted_iota(jnp.int32, (TOK, 128), 1)
    col_head = lax.broadcasted_iota(jnp.int32, (96, 256), 0) % 32
    col_lane = lax.broadcasted_iota(jnp.int32, (96, 256), 1) // 128

    def one_head(h, col_log):
        gap = jnp.where(causal, col_log - cumt[pl.ds(h, 1), :], NEG)
        return (gmat[...] * jnp.exp(gap) * step[pl.ds(h, 1), :]).astype(BF16)

    def intra(p, carry):
        h = 2 * p
        col = dot(cum3[...], (col_head == h + col_lane).astype(F32).astype(BF16))
        mixing = jnp.concatenate([one_head(h, col[:, :128]), one_head(h + 1, col[:, 128:])], axis=1)
        xp = xc[p]
        zero = jnp.zeros_like(xp)
        stacked = jnp.concatenate([jnp.where(lane < 64, xp, zero), jnp.where(lane < 64, zero, xp)], axis=0)
        lanes = pl.ds(pl.multiple_of(p * 128, 128), 128)
        g = silu(gate[:, lanes].astype(F32))
        ylocal[p] = (dot(mixing, stacked) + spx[p, 264:265] * xp.astype(F32)) * g
        egate[p] = spx[p, TOK : 2 * TOK] * g
        return carry

    loads[12].wait()
    loads[13].wait()
    take(0, 0)
    lax.fori_loop(0, 4, intra, 0, unroll=2)
    take(0, 1)
    lax.fori_loop(4, 10, intra, 0, unroll=2)
    take(1, 0)
    lax.fori_loop(10, 16, intra, 0, unroll=2)
    take(1, 1)

    log_scale = math.log2(math.e) / math.sqrt(128)
    rounds = ((0, 1, 7), (2, 6), (3, 5, 4))

    def tile(pos, kinds, offsets, edge):
        width = 256 * len(offsets)
        total = width * len(kinds)

        def load(kind):
            return jnp.concatenate(
                [
                    kvg[pl.ds((z + o) % 8 * 2, 2), pk, posk, kind].reshape(256, 128)
                    for pk, posk in kinds
                    for o in offsets
                ],
                axis=0,
            )

        kt = load(0)
        vt = jnp.concatenate([load(1), jnp.ones((total, 128), BF16)], axis=1)
        if edge:
            lanes = lax.broadcasted_iota(jnp.int32, (1, total), 1)
            key = jnp.full((1, total), -1, jnp.int32)
            for i, o in enumerate(offsets):
                here = (lanes // 256 == i + (total - width) // 256)
                key = jnp.where(here, (z + o) % 8 * 256 + lanes % 256, key)

        def scores(i):
            return dot(qb[pos, i * RC : i * RC + RC], kt, NT)

        ahead = scores(0)
        for i in range(ROWS // RC):
            cut = slice(i * RC, i * RC + RC)
            s = ahead
            if i + 1 < ROWS // RC:
                ahead = scores(i + 1)
            if edge:
                tok = (lax.broadcasted_iota(jnp.int32, (RC, total), 0) + i * RC) // 8
                s = jnp.where(key <= tok + r * 128, s, NEG)
            old = mrun[pos, cut]
            new = jnp.maximum(old, jnp.max(s, axis=1, keepdims=True))
            p = jnp.exp2((s - jnp.concatenate([new] * (total // 128), axis=1)) * log_scale)
            fade = jnp.exp2((old - new) * log_scale)
            acc[pos, cut] = acc[pos, cut] * jnp.concatenate([fade, fade], axis=1) + dot(p.astype(BF16), vt)
            mrun[pos, cut] = new

    def part_a(n):
        tile(1, ((0, 0), (1, 0)), rounds[n], False)

    def part_b(n):
        tile(1 - pr, ((1 - pr, 1 - pr), (pr, 1 - pr)), rounds[n], True)

    def part_c(n):
        tile(pr, ((pr, pr),), rounds[n], True)

    def close(pos):
        for i in range(ROWS // RC):
            cut = slice(i * RC, i * RC + RC)
            a = acc[pos, cut]
            obuf[pos, cut] = (a[:, :128] / a[:, 128:]).astype(BF16)

    mrun[...] = jnp.full((2, ROWS, 128), NEG, F32)
    acc[...] = jnp.zeros((2, ROWS, 256), F32)
    q_swap.wait()
    q_own.wait()
    for k in range(6):
        core_in[k].wait_recv()

    def chain(k, carry):
        state, logs = carry

        @pl.when(k != z)
        def _():
            remote(smsg.at[k], rmsg.at[k], a1s.at[k], a1r.at[k], dev(x, k * 2 + c)).wait_recv()

        pre[k] = state
        clog[k] = jnp.broadcast_to(logs, (8, 128))
        new = read_log(rmsg[k, NS:MSG])
        return jnp.exp(new) * state + rmsg[k, 0:NS].astype(F32), logs + new

    state, logs = lax.fori_loop(0, 8, chain, (jnp.zeros((NS, 128), F32), jnp.zeros((1, 128), F32)))
    xsend[0:NS] = state
    xsend[NS : NS + 8] = jnp.broadcast_to(logs, (8, 128))

    def x_copy(j):
        to = (x + j) % 4
        return remote(xsend, xrecv.at[x], xxs.at[to], xxr.at[x], dev(to, r))

    for j in range(1, 4):

        @pl.when(x + j < 4)
        def _():
            x_copy(j).start()


    part_a(0)
    take_ring(2)
    enter = jnp.zeros((NS, 128), F32)
    for j in range(3):

        @pl.when(x > j)
        def _():
            remote(xsend, xrecv.at[j], xxs.at[j], xxr.at[j], dev(j, r)).wait_recv()

    for j in range(3):
        enter = jnp.where(j < x, jnp.exp(xrecv[j, NS : NS + 1]) * enter + xrecv[j, 0:NS], enter)

    def back_copy(k):
        return remote(isend.at[k], iback.at[z], a2s.at[k], a2r.at[z], dev(x, k * 2 + c))

    def send_back(j, carry):
        k = (z + j) % 8
        isend[k] = jnp.exp(clog[k, 0:1]) * enter + pre[k]
        back_copy(k).start()
        return carry

    lax.fori_loop(1, 8, send_back, 0)
    iback[z] = jnp.exp(clog[z, 0:1]) * enter + pre[z]

    part_b(0)
    take_ring(3)
    part_c(0)
    for k in range(6, 10):
        core_in[k].wait_recv()
    part_a(1)
    take_side(2)
    take_side(3)
    part_b(1)
    part_c(1)

    def wait_back(j, carry):
        k = (z + j) % 8
        remote(isend.at[k], iback.at[k], a2s.at[k], a2r.at[k], dev(x, k * 2 + c)).wait_recv()
        return carry

    lax.fori_loop(1, 8, wait_back, 0)

    def hand_over(k, carry):
        before = iback[k]
        past = jnp.exp(read_log(both[0, k, NS:MSG])) * before + both[0, k, 0:NS].astype(F32)
        irecv[c, k] = jnp.where(c == 0, before, past)
        ipass[k] = jnp.where(c == 0, past, before)
        return carry

    lax.fori_loop(0, 8, hand_over, 0)
    state_swap = remote(ipass, irecv.at[c], bs.at[0], br.at[0], core)
    state_swap.start()

    for k in range(10, 18):
        core_in[k].wait_recv()

    o_swap = remote(obuf.at[1 - hi], oin, os_.at[0], or_.at[0], partner)

    def row_copy(j):
        to = (tp + j) % TP
        return remote(nbuf.at[to], nrecv.at[tp], tps.at[to], tpr.at[tp], (ctx, to))

    def finish_all():
        state_swap.wait()

        def finish(p, square):
            state = irecv[p % 2, p // 2]
            top = state.astype(BF16)
            low = (state - top.astype(F32)).astype(BF16)
            y = ylocal[p] + egate[p] * dot(twice, jnp.concatenate([top, low], axis=0))
            ylocal[p] = y
            return square + y * y

        twice = jnp.concatenate([bcv[1], bcv[1]], axis=1)
        square = lax.fori_loop(0, PAIRS, finish, jnp.zeros((TOK, 128), F32), unroll=4)
        norm = lax.rsqrt(jnp.sum(square, axis=1, keepdims=True) * (1.0 / 2048) + NORM_EPS)

        def scale(p, carry):
            lanes = pl.ds(pl.multiple_of(p * 128, 128), 128)
            v = (ylocal[p] * norm * gain[:, lanes]).astype(BF16)
            for k in range(TP):
                nbuf[k, :, lanes] = v[k * 32 : k * 32 + 32]
            return carry

        lax.fori_loop(0, PAIRS, scale, 0, unroll=4)

        for j in range(1, TP):
            row_copy(j).start()
        nrecv[tp] = nbuf[tp]

    def last_round(it, carry):
        is_a = it == hi
        other1 = jnp.where(hi == 0, it == 1, it == 2)
        other0 = jnp.where(hi == 0, it == 2, it == 0)
        is_b = jnp.where(pr == 0, other1, other0)
        is_c = jnp.where(pr == 0, other0, other1)

        @pl.when(it == 1)
        def _():
            finish_all()

        @pl.when(is_a)
        def _():
            part_a(2)

        @pl.when(is_b)
        def _():
            part_b(2)

        @pl.when(is_c)
        def _():
            part_c(2)

        @pl.when(it == 1 - hi)
        def _():
            close(1 - hi)
            o_swap.start()

        return carry

    lax.fori_loop(0, 3, last_round, 0)
    close(hi)

    for j in range(1, TP):
        k = (tp + j) % TP
        remote(nbuf.at[k], nrecv.at[k], tps.at[k], tpr.at[k], (ctx, k)).wait_recv()
    for k in range(TP):
        out[:, k * 2048 : (k + 1) * 2048] = nrecv[k].astype(F32)

    def left_group(j, carry):
        k = (z + j) % 8
        state_copy(k).wait_send()
        back_copy(k).wait_send()
        return carry

    lax.fori_loop(1, 8, left_group, 0)
    for j in range(1, 4):

        @pl.when(x + j < 4)
        def _():
            x_copy(j).wait_send()

        row_copy(j).wait_send()
    for copy in sends:
        copy.wait_send()
    o_swap.wait()
    here = obuf[hi].astype(F32).reshape(TOK, 8, 128)
    there = oin[...].astype(F32).reshape(TOK, 8, 128)
    first_heads = jnp.where(hi == 0, here, there)
    last_heads = jnp.where(hi == 0, there, here)
    att[...] = jnp.concatenate([first_heads, last_heads], axis=1).astype(BF16)


def per_device(
    mamba_x, bc_in, gate_z, conv_x_weight, conv_x_bias, conv_bc_weight, conv_bc_bias,
    decay_log, step_size, d_skip, norm_gain, queries, attn_keys, attn_values,
):
    args = (
        mamba_x, bc_in, gate_z, conv_x_weight, conv_x_bias.reshape(1, 2048), conv_bc_weight, conv_bc_bias,
        decay_log.T, step_size.T, d_skip.reshape(1, 32), norm_gain.reshape(1, 2048), queries, attn_keys, attn_values,
    )
    vmem = pl.BlockSpec(memory_space=pltpu.VMEM)
    dma = lambda *n: pltpu.SemaphoreType.DMA(n)
    buf = pltpu.VMEM
    msgs = (8, MSG, 128)
    out, att = pl.pallas_call(
        body,
        out_shape=(
            jax.ShapeDtypeStruct((32, 8192), F32),
            jax.ShapeDtypeStruct((TOK, 16, 128), BF16),
        ),
        in_specs=[pl.BlockSpec(memory_space=pltpu.HBM)] * 14,
        out_specs=(vmem, vmem),
        scratch_shapes=[buf(a.shape, a.dtype) for a in args]
        + [
            buf((2, ROWS, 128), BF16), buf((2, 2, TOK, 128), BF16),
            buf((16, 2048), BF16), buf((16, 2, 128), BF16), buf((144, 128), F32), buf((PAIRS, TOK, 128), BF16),
            buf((2, TOK, 128), BF16), buf((NS, TOK), BF16), buf((32, TOK), F32),
            buf((TOK, 96), BF16), buf((PAIRS, 272, 128), F32), buf((TOK, TOK), F32),
            buf((PAIRS, TOK, 128), F32), buf((PAIRS, TOK, 128), F32),
            buf(msgs, BF16), buf((2,) + msgs, BF16), buf(msgs, BF16), buf(msgs, BF16),
            buf((8, NS, 128), F32), buf((8, 8, 128), F32), buf((NS + 8, 128), F32), buf((4, NS + 8, 128), F32),
            buf((8, NS, 128), F32), buf((8, NS, 128), F32), buf((8, NS, 128), F32), buf((2, 8, NS, 128), F32),
            buf((2, ROWS, 128), BF16), buf((16, 2, 2, 2, 128, 128), BF16), buf((2, ROWS, 256), F32),
            buf((2, ROWS, 128), F32), buf((2, ROWS, 128), BF16), buf((ROWS, 128), BF16), buf((TP, 32, 2048), BF16), buf((TP, 32, 2048), BF16),
            dma(17), dma(4), dma(4), dma(1), dma(1), dma(12), dma(12), dma(18), dma(18), dma(4), dma(4), dma(1), dma(1),
            dma(8), dma(8), dma(4), dma(4), dma(8), dma(8), dma(1), dma(1), dma(TP), dma(TP), dma(1), dma(1),
        ],
        compiler_params=pltpu.CompilerParams(
            collective_id=0, has_side_effects=True, vmem_limit_bytes=60 << 20
        ),
    )(*args)
    return out, att


def solution(mesh):
    in_specs = (
        P("ctx", "tp"), P("ctx", None, "tp"), P("ctx", "tp"), P(None, "tp"), P("tp"), P(None, None, "tp"),
        P(None, "tp"), P("ctx", "tp"), P("ctx", "tp"), P("tp"), P("tp"), P("ctx", "tp", None),
        P("ctx", "tp", None), P("ctx", "tp", None),
    )
    out_specs = (P(("ctx", "tp"), None), P("ctx", "tp", None))
    return jax.shard_map(per_device, mesh=mesh, in_specs=in_specs, out_specs=out_specs, check_vma=False)
```

```python
import functools
import math

import jax
import jax.numpy as jnp
from jax import lax
from jax.experimental import pallas as pl
from jax.experimental.pallas import tpu as pltpu
from jax.sharding import PartitionSpec as P

MESH = pl.DeviceIdType.MESH
F32 = jnp.float32
BF16 = jnp.bfloat16
EXACT = lax.Precision.HIGHEST

TOK = 128
NS = 128
PAIRS = 16
TP = 4
ROWS = 1024
RC = 256
NEG = -1e30
NORM_EPS = 1e-05
MSG = 144

NT = (((1,), (1,)), ((), ()))


def dot(a, b, dims=(((1,), (0,)), ((), ())), precision=None):
    return lax.dot_general(a, b, dims, precision=precision, preferred_element_type=F32)


def silu(v):
    return v * jax.nn.sigmoid(v)


def split3(v):
    top = v.astype(BF16)
    rest = v - top.astype(F32)
    mid = rest.astype(BF16)
    low = (rest - mid.astype(F32)).astype(BF16)
    return top, mid, low


def body(
    mx_, bc_, gate_, wx_, bx_, wbc_, bbc_, decay_, step_, dskip_, gain_, q_, k_, v_,
    out, att,
    mx, bc, gate, wx, bx, wbc, bbc, decay, step, dskip, gain, q, kin, vin, q2, kvp,
    hx, hbc, win, xc, bcv, btr, cumt, cum3, spx, gmat, ylocal, egate,
    other, both, smsg, rmsg, pre, clog, xsend, xrecv, isend, iback, ipass, irecv,
    qb, kvg, acc, mrun, obuf, oin, nbuf, nrecv,
    loc, sws, swr, xs, xr, rs, rr, cs, cr, fs, fr, ms, mr, a1s, a1r, xxs, xxr, a2s, a2r, bs, br, tps, tpr, os_, or_,
):
    ctx, tp = lax.axis_index("ctx"), lax.axis_index("tp")
    x, r = ctx // 16, ctx % 16
    z, c = r // 2, r % 2
    hi = x // 2
    px = 3 - x
    pr = x + hi * (3 - 2 * x)
    xn = x + 1 - 2 * (x % 2)
    zp, zm = (z + 1) % 8, (z + 7) % 8

    def dev(x_, r_):
        return (x_ * 16 + r_, tp)

    def remote(src, dst, s, rv, to):
        return pltpu.make_async_remote_copy(
            src_ref=src, dst_ref=dst, send_sem=s, recv_sem=rv, device_id=to, device_id_type=MESH
        )

    def local(src, dst, k):
        return pltpu.make_async_copy(src, dst, loc.at[k])

    bar = pltpu.get_barrier_semaphore()

    def greet(to):
        pl.semaphore_signal(bar, inc=1, device_id=to, device_id_type=MESH)

    for j in range(1, 8):
        greet(dev(x, (z + j) % 8 * 2 + c))
    for j in range(1, 4):
        greet(dev((x + j) % 4, r))
        greet((ctx, (tp + j) % 4))
    greet(dev(x, z * 2 + 1 - c))
    greet(((ctx + 1) % 64, tp))
    greet(((ctx + 63) % 64, tp))

    brought = (
        (k_, kin), (v_, vin), (decay_, decay), (step_, step), (dskip_, dskip), (q_, q), (bc_, bc), (mx_, mx), (wx_, wx),
        (bx_, bx), (wbc_, wbc), (bbc_, bbc), (gate_, gate), (gain_, gain),
    )
    loads = [local(a, b, k) for k, (a, b) in enumerate(brought)]
    for load in loads:
        load.start()
    loads[0].wait()
    loads[1].wait()
    for k, part in enumerate((kin, vin)):
        part = part[...].astype(F32)
        for j in range(2):
            kvp[j, k] = part[:, j].astype(BF16)
    kv_own = local(kvp.at[hi], kvg.at[r, pr, hi], 14)
    kv_own.start()
    pl.semaphore_wait(bar, 16)

    partner = dev(px, r)
    core = dev(x, z * 2 + 1 - c)
    mine = kvg.at[r, pr]
    after = ((ctx + 1) % 64, tp)
    halo_x = remote(mx_.at[TOK - 16 : TOK], hx, sws.at[1], swr.at[1], after)
    halo_x.start()
    halo_bc = remote(bc_.at[TOK - 16 : TOK], hbc, sws.at[2], swr.at[2], after)
    halo_bc.start()
    kv_swap = remote(kvp.at[1 - hi], kvg.at[r, pr, hi], sws.at[0], swr.at[0], partner)
    kv_swap.start()
    loads[5].wait()
    heads = q[...].astype(F32)
    for j in range(2):
        q2[j] = heads[:, 8 * j : 8 * j + 8].reshape(ROWS, 128).astype(BF16)
    q_own = local(q2.at[hi], qb.at[hi], 15)
    q_own.start()
    q_swap = remote(q2.at[1 - hi], qb.at[hi], sws.at[3], swr.at[3], partner)
    q_swap.start()

    rows = lax.broadcasted_iota(jnp.int32, (TOK, TOK), 0)
    cols = lax.broadcasted_iota(jnp.int32, (TOK, TOK), 1)
    causal = rows >= cols
    loads[2].wait()
    loads[3].wait()
    tril = causal.astype(F32)
    cum = dot(tril, decay[...], NT, EXACT)
    cumt[...] = dot(decay[...], tril, NT, EXACT)
    last = cum[TOK - 1 : TOK]
    wend = jnp.exp(last - cum) * dot((rows == cols).astype(F32), step[...], NT, EXACT)
    cum3[...] = jnp.concatenate(split3(cum), axis=1)
    loads[4].wait()
    wide = jnp.concatenate(
        [wend, jnp.exp(cum), jnp.broadcast_to(last, (8, 32)), jnp.broadcast_to(dskip[...], (8, 32))], axis=0
    )
    wide = jnp.concatenate(split3(wide), axis=1)
    for k in range(4):
        head = lax.broadcasted_iota(jnp.int32, (96, 512), 0) % 32
        lane_head = (lax.broadcasted_iota(jnp.int32, (96, 512), 1) + 512 * k) // 64
        part = dot(wide, (head == lane_head).astype(F32).astype(BF16))
        for j in range(4):
            spx[4 * k + j] = part[:, j * 128 : (j + 1) * 128]

    sends = []

    def ring(slot, d, k):
        copy = remote(slot, slot, rs.at[k], rr.at[k], dev(x, (zp if d == 0 else zm) * 2 + c))
        copy.start()
        sends.append(copy)
        return copy

    def pass_on(slot, k, s, rv, to):
        copy = remote(slot, slot, s.at[k], rv.at[k], to)
        copy.start()
        sends.append(copy)
        return copy

    core_in = {}

    def to_core(slot, k):
        core_in[k] = pass_on(slot, k, cs, cr, core)

    hops = {}
    kv_own.wait()
    kv_swap.wait()
    x_swap = remote(mine, mine, xs.at[0], xr.at[0], dev(xn, r))
    x_swap.start()
    hops[0, 0, 0] = ring(mine, 0, 0)
    hops[1, 0, 0] = ring(mine, 1, 1)
    to_core(mine, 0)

    for k in range(6, 12):
        loads[k].wait()
    halo_x.wait()
    halo_bc.wait()
    first = ctx > 0

    def conv(chunk, before, weight, bias):
        win[0:16] = jnp.where(first, before.astype(F32), 0.0)
        win[16:144] = chunk.astype(F32)
        w = weight.astype(F32)
        total = jnp.broadcast_to(bias, (TOK, 128))
        for k in range(4):
            total = total + win[13 + k : 13 + k + TOK] * w[k : k + 1]
        return silu(total).astype(BF16)

    for k in range(2):
        bcv[k] = conv(
            bc[...].astype(F32)[:, k], hbc[...].astype(F32)[:, k], wbc[...].astype(F32)[:, k], bbc[k : k + 1]
        )
    btr[...] = bcv[0].astype(F32).T.astype(BF16)

    def conv_pair(p, carry):
        cut = pl.ds(pl.multiple_of(p * 128, 128), 128)
        xc[p] = conv(mx[:, cut], hx[:, cut], wx[:, cut], bx[:, cut])
        return carry

    lax.fori_loop(0, PAIRS, conv_pair, 0)

    row16 = lax.broadcasted_iota(jnp.int32, (16, 128), 0)

    def log_rows(v):
        top, mid, low = split3(jnp.broadcast_to(v, (16, 128)))
        zero = jnp.zeros((16, 128), BF16)
        return jnp.where(row16 == 0, top, jnp.where(row16 == 1, mid, jnp.where(row16 == 2, low, zero)))

    def read_log(msg_tail):
        v = msg_tail.astype(F32)
        return v[0:1] + v[1:2] + v[2:3]

    def local_state(p):
        weighted = (xc[p].astype(F32) * spx[p, 0:TOK]).astype(BF16)
        return dot(btr[...], weighted).astype(BF16), log_rows(spx[p, 256:257])

    def state_for_core(k, carry):
        state, logs = local_state(2 * k + 1 - c)
        other[k, 0:NS] = state
        other[k, NS:MSG] = logs
        return carry

    lax.fori_loop(0, 8, state_for_core, 0, unroll=4)
    core_swap = remote(other, both.at[c], ms.at[0], mr.at[0], core)
    core_swap.start()
    x_swap.wait()
    theirs = kvg.at[r, 1 - pr]
    hops[0, 0, 1] = ring(theirs, 0, 2)
    hops[1, 0, 1] = ring(theirs, 1, 3)
    to_core(theirs, 1)

    def state_own(k, carry):
        state, logs = local_state(2 * k + c)
        both[c, k, 0:NS] = state
        both[c, k, NS:MSG] = logs
        return carry

    lax.fori_loop(0, 8, state_own, 0, unroll=4)
    core_swap.wait()

    def state_copy(k):
        return remote(smsg.at[k], rmsg.at[z], a1s.at[k], a1r.at[z], dev(x, k * 2 + c))

    def chip_state(k):
        log0, log1 = read_log(both[0, k, NS:MSG]), read_log(both[1, k, NS:MSG])
        state = jnp.exp(log1) * both[0, k, 0:NS].astype(F32) + both[1, k, 0:NS].astype(F32)
        return state.astype(BF16), log_rows(log0 + log1)

    def send_state(j, carry):
        k = (z + j) % 8
        state, logs = chip_state(k)
        smsg[k, 0:NS] = state
        smsg[k, NS:MSG] = logs
        state_copy(k).start()
        return carry

    lax.fori_loop(1, 8, send_state, 0)
    state, logs = chip_state(z)
    rmsg[z, 0:NS] = state
    rmsg[z, NS:MSG] = logs

    def slot_at(zo, q):
        return kvg.at[zo % 8 * 2 + c, pr if q == 0 else 1 - pr]

    def source(d, s):
        return z + 7 - s if d == 0 else z + s + 1

    def take(s, q):
        for d in range(2):
            hops[d, s, q].wait_recv()
            slot = slot_at(source(d, s), q)
            if s == 0 or q == 0:
                hops[d, s + 1, q] = ring(slot, d, 4 + s * 4 + q * 2 + d)
            to_core(slot, 2 + s * 4 + q * 2 + d)

    def take_ring(s):
        for d in range(2):
            hops[d, s, 0].wait_recv()
            slot = slot_at(source(d, s), 0)
            if s == 2:
                hops[d, 3, 0] = ring(slot.at[d], d, 10 + d)
            else:
                slot = slot.at[d]
            side[s, d] = pass_on(slot, (s - 2) * 2 + d, fs, fr, dev(xn, r))
            to_core(slot, 10 + (s - 2) * 4 + d)

    side = {}

    def take_side(s):
        for d in range(2):
            side[s, d].wait_recv()
            slot = slot_at(source(d, s), 1)
            to_core(slot if s == 2 else slot.at[d], 12 + (s - 2) * 4 + d)

    gmat[...] = dot(bcv[1], bcv[0], NT)
    lane = lax.broadcasted_iota(jnp.int32, (TOK, 128), 1)
    col_head = lax.broadcasted_iota(jnp.int32, (96, 256), 0) % 32
    col_lane = lax.broadcasted_iota(jnp.int32, (96, 256), 1) // 128

    def one_head(h, col_log):
        gap = jnp.where(causal, col_log - cumt[pl.ds(h, 1), :], NEG)
        return (gmat[...] * jnp.exp(gap) * step[pl.ds(h, 1), :]).astype(BF16)

    def intra(p, carry):
        h = 2 * p
        col = dot(cum3[...], (col_head == h + col_lane).astype(F32).astype(BF16))
        mixing = jnp.concatenate([one_head(h, col[:, :128]), one_head(h + 1, col[:, 128:])], axis=1)
        xp = xc[p]
        zero = jnp.zeros_like(xp)
        stacked = jnp.concatenate([jnp.where(lane < 64, xp, zero), jnp.where(lane < 64, zero, xp)], axis=0)
        lanes = pl.ds(pl.multiple_of(p * 128, 128), 128)
        g = silu(gate[:, lanes].astype(F32))
        ylocal[p] = (dot(mixing, stacked) + spx[p, 264:265] * xp.astype(F32)) * g
        egate[p] = spx[p, TOK : 2 * TOK] * g
        return carry

    loads[12].wait()
    loads[13].wait()
    take(0, 0)
    lax.fori_loop(0, 4, intra, 0, unroll=2)
    take(0, 1)
    lax.fori_loop(4, 10, intra, 0, unroll=2)
    take(1, 0)
    lax.fori_loop(10, 16, intra, 0, unroll=2)
    take(1, 1)

    log_scale = math.log2(math.e) / math.sqrt(128)
    rounds = ((0, 1, 7), (2, 6), (3, 5, 4))

    def tile(pos, kinds, offsets, edge):
        width = 256 * len(offsets)
        total = width * len(kinds)

        def load(kind):
            return jnp.concatenate(
                [
                    kvg[pl.ds((z + o) % 8 * 2, 2), pk, posk, kind].reshape(256, 128)
                    for pk, posk in kinds
                    for o in offsets
                ],
                axis=0,
            )

        kt = load(0)
        vt = jnp.concatenate([load(1), jnp.ones((total, 128), BF16)], axis=1)
        if edge:
            lanes = lax.broadcasted_iota(jnp.int32, (1, total), 1)
            key = jnp.full((1, total), -1, jnp.int32)
            for i, o in enumerate(offsets):
                here = (lanes // 256 == i + (total - width) // 256)
                key = jnp.where(here, (z + o) % 8 * 256 + lanes % 256, key)

        def scores(i):
            return dot(qb[pos, i * RC : i * RC + RC], kt, NT)

        ahead = scores(0)
        for i in range(ROWS // RC):
            cut = slice(i * RC, i * RC + RC)
            s = ahead
            if i + 1 < ROWS // RC:
                ahead = scores(i + 1)
            if edge:
                tok = (lax.broadcasted_iota(jnp.int32, (RC, total), 0) + i * RC) // 8
                s = jnp.where(key <= tok + r * 128, s, NEG)
            old = mrun[pos, cut]
            new = jnp.maximum(old, jnp.max(s, axis=1, keepdims=True))
            p = jnp.exp2((s - jnp.concatenate([new] * (total // 128), axis=1)) * log_scale)
            fade = jnp.exp2((old - new) * log_scale)
            acc[pos, cut] = acc[pos, cut] * jnp.concatenate([fade, fade], axis=1) + dot(p.astype(BF16), vt)
            mrun[pos, cut] = new

    def part_a(n):
        tile(1, ((0, 0), (1, 0)), rounds[n], False)

    def part_b(n):
        tile(1 - pr, ((1 - pr, 1 - pr), (pr, 1 - pr)), rounds[n], True)

    def part_c(n):
        tile(pr, ((pr, pr),), rounds[n], True)

    def close(pos):
        for i in range(ROWS // RC):
            cut = slice(i * RC, i * RC + RC)
            a = acc[pos, cut]
            obuf[pos, cut] = (a[:, :128] / a[:, 128:]).astype(BF16)

    mrun[...] = jnp.full((2, ROWS, 128), NEG, F32)
    acc[...] = jnp.zeros((2, ROWS, 256), F32)
    q_swap.wait()
    q_own.wait()
    for k in range(6):
        core_in[k].wait_recv()

    def chain(k, carry):
        state, logs = carry

        @pl.when(k != z)
        def _():
            remote(smsg.at[k], rmsg.at[k], a1s.at[k], a1r.at[k], dev(x, k * 2 + c)).wait_recv()

        pre[k] = state
        clog[k] = jnp.broadcast_to(logs, (8, 128))
        new = read_log(rmsg[k, NS:MSG])
        return jnp.exp(new) * state + rmsg[k, 0:NS].astype(F32), logs + new

    state, logs = lax.fori_loop(0, 8, chain, (jnp.zeros((NS, 128), F32), jnp.zeros((1, 128), F32)))
    xsend[0:NS] = state
    xsend[NS : NS + 8] = jnp.broadcast_to(logs, (8, 128))

    def x_copy(j):
        to = (x + j) % 4
        return remote(xsend, xrecv.at[x], xxs.at[to], xxr.at[x], dev(to, r))

    for j in range(1, 4):

        @pl.when(x + j < 4)
        def _():
            x_copy(j).start()


    part_a(0)
    take_ring(2)
    enter = jnp.zeros((NS, 128), F32)
    for j in range(3):

        @pl.when(x > j)
        def _():
            remote(xsend, xrecv.at[j], xxs.at[j], xxr.at[j], dev(j, r)).wait_recv()

    for j in range(3):
        enter = jnp.where(j < x, jnp.exp(xrecv[j, NS : NS + 1]) * enter + xrecv[j, 0:NS], enter)

    def back_copy(k):
        return remote(isend.at[k], iback.at[z], a2s.at[k], a2r.at[z], dev(x, k * 2 + c))

    def send_back(j, carry):
        k = (z + j) % 8
        isend[k] = jnp.exp(clog[k, 0:1]) * enter + pre[k]
        back_copy(k).start()
        return carry

    lax.fori_loop(1, 8, send_back, 0)
    iback[z] = jnp.exp(clog[z, 0:1]) * enter + pre[z]

    part_b(0)
    take_ring(3)
    part_c(0)
    for k in range(6, 10):
        core_in[k].wait_recv()
    part_a(1)
    take_side(2)
    take_side(3)
    part_b(1)
    part_c(1)

    def wait_back(j, carry):
        k = (z + j) % 8
        remote(isend.at[k], iback.at[k], a2s.at[k], a2r.at[k], dev(x, k * 2 + c)).wait_recv()
        return carry

    lax.fori_loop(1, 8, wait_back, 0)

    def hand_over(k, carry):
        before = iback[k]
        past = jnp.exp(read_log(both[0, k, NS:MSG])) * before + both[0, k, 0:NS].astype(F32)
        irecv[c, k] = jnp.where(c == 0, before, past)
        ipass[k] = jnp.where(c == 0, past, before)
        return carry

    lax.fori_loop(0, 8, hand_over, 0)
    state_swap = remote(ipass, irecv.at[c], bs.at[0], br.at[0], core)
    state_swap.start()

    for k in range(10, 18):
        core_in[k].wait_recv()

    o_swap = remote(obuf.at[1 - hi], oin, os_.at[0], or_.at[0], partner)

    def row_copy(j):
        to = (tp + j) % TP
        return remote(nbuf.at[to], nrecv.at[tp], tps.at[to], tpr.at[tp], (ctx, to))

    def finish_all():
        state_swap.wait()

        def finish(p, square):
            state = irecv[p % 2, p // 2]
            top = state.astype(BF16)
            low = (state - top.astype(F32)).astype(BF16)
            y = ylocal[p] + egate[p] * dot(twice, jnp.concatenate([top, low], axis=0))
            ylocal[p] = y
            return square + y * y

        twice = jnp.concatenate([bcv[1], bcv[1]], axis=1)
        square = lax.fori_loop(0, PAIRS, finish, jnp.zeros((TOK, 128), F32), unroll=4)
        norm = lax.rsqrt(jnp.sum(square, axis=1, keepdims=True) * (1.0 / 2048) + NORM_EPS)

        def scale(p, carry):
            lanes = pl.ds(pl.multiple_of(p * 128, 128), 128)
            v = (ylocal[p] * norm * gain[:, lanes]).astype(BF16)
            for k in range(TP):
                nbuf[k, :, lanes] = v[k * 32 : k * 32 + 32]
            return carry

        lax.fori_loop(0, PAIRS, scale, 0, unroll=4)

        for j in (2, 1, 3):
            row_copy(j).start()
        nrecv[tp] = nbuf[tp]

    def last_round(it, carry):
        is_a = it == hi
        other1 = jnp.where(hi == 0, it == 1, it == 2)
        other0 = jnp.where(hi == 0, it == 2, it == 0)
        is_b = jnp.where(pr == 0, other1, other0)
        is_c = jnp.where(pr == 0, other0, other1)

        @pl.when(it == 2 - hi)
        def _():
            finish_all()

        @pl.when(is_a)
        def _():
            part_a(2)

        @pl.when(is_b)
        def _():
            part_b(2)

        @pl.when(is_c)
        def _():
            part_c(2)

        @pl.when(it == 1 - hi)
        def _():
            close(1 - hi)
            o_swap.start()

        return carry

    lax.fori_loop(0, 3, last_round, 0)
    close(hi)

    for j in range(1, TP):
        k = (tp + j) % TP
        remote(nbuf.at[k], nrecv.at[k], tps.at[k], tpr.at[k], (ctx, k)).wait_recv()
    for k in range(TP):
        out[:, k * 2048 : (k + 1) * 2048] = nrecv[k].astype(F32)

    def left_group(j, carry):
        k = (z + j) % 8
        state_copy(k).wait_send()
        back_copy(k).wait_send()
        return carry

    lax.fori_loop(1, 8, left_group, 0)
    for j in range(1, 4):

        @pl.when(x + j < 4)
        def _():
            x_copy(j).wait_send()

        row_copy(j).wait_send()
    for copy in sends:
        copy.wait_send()
    o_swap.wait()
    here = obuf[hi].astype(F32).reshape(TOK, 8, 128)
    there = oin[...].astype(F32).reshape(TOK, 8, 128)
    first_heads = jnp.where(hi == 0, here, there)
    last_heads = jnp.where(hi == 0, there, here)
    att[...] = jnp.concatenate([first_heads, last_heads], axis=1).astype(BF16)


def per_device(
    mamba_x, bc_in, gate_z, conv_x_weight, conv_x_bias, conv_bc_weight, conv_bc_bias,
    decay_log, step_size, d_skip, norm_gain, queries, attn_keys, attn_values,
):
    args = (
        mamba_x, bc_in, gate_z, conv_x_weight, conv_x_bias.reshape(1, 2048), conv_bc_weight, conv_bc_bias,
        decay_log.T, step_size.T, d_skip.reshape(1, 32), norm_gain.reshape(1, 2048), queries, attn_keys, attn_values,
    )
    vmem = pl.BlockSpec(memory_space=pltpu.VMEM)
    dma = lambda *n: pltpu.SemaphoreType.DMA(n)
    buf = pltpu.VMEM
    msgs = (8, MSG, 128)
    out, att = pl.pallas_call(
        body,
        out_shape=(
            jax.ShapeDtypeStruct((32, 8192), F32),
            jax.ShapeDtypeStruct((TOK, 16, 128), BF16),
        ),
        in_specs=[pl.BlockSpec(memory_space=pltpu.HBM)] * 14,
        out_specs=(vmem, vmem),
        scratch_shapes=[buf(a.shape, a.dtype) for a in args]
        + [
            buf((2, ROWS, 128), BF16), buf((2, 2, TOK, 128), BF16),
            buf((16, 2048), BF16), buf((16, 2, 128), BF16), buf((144, 128), F32), buf((PAIRS, TOK, 128), BF16),
            buf((2, TOK, 128), BF16), buf((NS, TOK), BF16), buf((32, TOK), F32),
            buf((TOK, 96), BF16), buf((PAIRS, 272, 128), F32), buf((TOK, TOK), F32),
            buf((PAIRS, TOK, 128), F32), buf((PAIRS, TOK, 128), F32),
            buf(msgs, BF16), buf((2,) + msgs, BF16), buf(msgs, BF16), buf(msgs, BF16),
            buf((8, NS, 128), F32), buf((8, 8, 128), F32), buf((NS + 8, 128), F32), buf((4, NS + 8, 128), F32),
            buf((8, NS, 128), F32), buf((8, NS, 128), F32), buf((8, NS, 128), F32), buf((2, 8, NS, 128), F32),
            buf((2, ROWS, 128), BF16), buf((16, 2, 2, 2, 128, 128), BF16), buf((2, ROWS, 256), F32),
            buf((2, ROWS, 128), F32), buf((2, ROWS, 128), BF16), buf((ROWS, 128), BF16), buf((TP, 32, 2048), BF16), buf((TP, 32, 2048), BF16),
            dma(17), dma(4), dma(4), dma(1), dma(1), dma(12), dma(12), dma(18), dma(18), dma(4), dma(4), dma(1), dma(1),
            dma(8), dma(8), dma(4), dma(4), dma(8), dma(8), dma(1), dma(1), dma(TP), dma(TP), dma(1), dma(1),
        ],
        compiler_params=pltpu.CompilerParams(
            collective_id=0, has_side_effects=True, vmem_limit_bytes=60 << 20
        ),
    )(*args)
    return out, att


def solution(mesh):
    in_specs = (
        P("ctx", "tp"), P("ctx", None, "tp"), P("ctx", "tp"), P(None, "tp"), P("tp"), P(None, None, "tp"),
        P(None, "tp"), P("ctx", "tp"), P("ctx", "tp"), P("tp"), P("tp"), P("ctx", "tp", None),
        P("ctx", "tp", None), P("ctx", "tp", None),
    )
    out_specs = (P(("ctx", "tp"), None), P("ctx", "tp", None))
    return jax.shard_map(per_device, mesh=mesh, in_specs=in_specs, out_specs=out_specs, check_vma=False)
```
